32 devices in a mesh: dp: 4 (over x, core), context: 2 (over y), tensor: 4 (over z).
Axes of the slice: x: 2, y: 2, z: 4, core: 2. Of those that a mesh axis runs over, the one named last changes fastest.
Arguments:
- grad_out: bfloat16 [4096, 8192], P(('dp', 'context', 'tensor')), may hold values from -6 to 6
- queries: bfloat16 [4096, 1024], P(('dp', 'context'), 'tensor'), may hold values from -6 to 6
- attended: bfloat16 [4096, 1024], P(('dp', 'context'), 'tensor'), may hold values from -6 to 6
- keys: bfloat16 [4096, 128], P(('dp', 'context')), may hold values from -6 to 6
- values: bfloat16 [4096, 128], P(('dp', 'context')), may hold values from -6 to 6
- log_sums: float32 [8, 4096], P('tensor', ('dp', 'context')), may hold values from 1 to 3
- segment_ids: int32 [4, 1024], P('dp'), may hold values from 0 to 7, as said below
- w_out: bfloat16 [8192, 1024], P(('dp', 'context'), 'tensor'), may hold values from -0.0625 to 0.0625
- w_query: bfloat16 [1024, 8192], P('tensor', ('dp', 'context')), may hold values from -0.1875 to 0.1875
- w_key: bfloat16 [128, 8192], replicated, may hold values from -0.5 to 0.5
- w_value: bfloat16 [128, 8192], replicated, may hold values from -0.5 to 0.5
Outputs:
- grad_input: bfloat16 [4096, 8192], P(('dp', 'context', 'tensor'))
- out_proj_grad: float32 [8192, 1024], P(('dp', 'context'), 'tensor')
The draws below stay inside these ranges and needn't reach their ends.
Inputs may be any that keep to these rules, and one draw needn't show every extreme that they name: `segment_ids`: along the positions of a sequence the document number never falls; every sequence holds exactly 8 documents, numbered from 0.
All inputs are finite; a program needn't handle non-finite values.
Results may differ from the reference program's by a relative error of at most 0.02.
Values may be sent and summed in bfloat16 or wider, within the bound.
No kernel may reach another device: no remote copies, remote signals or barrier semaphores. Data moves between devices by JAX's collectives and lax.ppermute only.
A program may use at most 128 MiB of HBM per device.

```python
import math
import jax
import jax.numpy as jnp
from jax import lax

D = 8192
HQ = 8
HEAD = 128
DOCS = 8
SPAN = 256
LENGTH = 1024
SEQS = 4
TOKENS = 4096
N_CONTEXT = 2
N_TENSOR = 4


def draw_segment_ids(key, part):
    seq_keys = jax.random.split(jax.random.fold_in(key, 17), SEQS)

    def one_sequence(seq_key):
        cuts = jax.random.permutation(seq_key, LENGTH - 1)[:DOCS - 1] + 1
        positions = jnp.arange(LENGTH, dtype=jnp.int32)
        return jnp.sum((positions[:, None] >= cuts[None, :]).astype(jnp.int32), axis=1).astype(jnp.int32)
    return jax.vmap(one_sequence)(seq_keys)


def raised(array, stream_key, source, target, parts, factor):
    def block_of(axis_at):
        return (jnp.arange(array.shape[axis_at]) // (array.shape[axis_at] // parts)).reshape((-1,) + (1,) * (array.ndim - 1 - axis_at))

    near = jax.random.permutation(stream_key, parts)[block_of(target)]
    second = (block_of(target) + parts // 2) % parts
    return jnp.where((block_of(source) == near) | (block_of(source) == second), factor * array, array)


def level_of(own_key, extent, cuts, least, largest):
    level, own = 1.0, jax.random.fold_in(own_key, 6)
    for position, parts in cuts:
        steps = jnp.exp(jax.random.uniform(jax.random.fold_in(own, position), (parts,), jnp.float32, least / len(cuts), largest / len(cuts)))
        level = level * jnp.repeat(steps, extent[position] // parts).reshape([-1 if axis == position else 1 for axis in range(len(extent))])
    return level


def centred(key, dims, scale, reach, cuts=(), held_as=jnp.bfloat16):
    values = scale * jax.random.normal(key, dims, jnp.float32)
    if cuts:
        values = values * level_of(key, dims, cuts, -0.22, 0.18)
    return jnp.clip(values, -reach, reach).astype(held_as)


def gaussian_with(stream_key, dims, scale, reach, shards, heavy, kind=jnp.bfloat16):
    entries = scale * jax.random.normal(stream_key, dims, jnp.float32)
    if shards:
        entries = entries * level_of(stream_key, dims, shards, -0.22, 0.18)
    return jnp.clip(raised(entries, jax.random.fold_in(stream_key, 3), *heavy), -reach, reach).astype(kind)


def setup_inputs(seed: int = 0) -> dict:
    arg_keys = jax.random.split(jax.random.key(seed), 12)
    return {
        "grad_out": gaussian_with(arg_keys[0], (TOKENS, D), 1.0, 6.0, ((0, 32),), (0, 1, 32, 2.75)),
        "queries": centred(arg_keys[1], (TOKENS, HQ * HEAD), 1.0, 6.0, ((0, 8), (1, 4))),
        "attended": centred(arg_keys[2], (TOKENS, HQ * HEAD), 1.0, 6.0, ((0, 8), (1, 4))),
        "keys": centred(arg_keys[3], (TOKENS, HEAD), 1.0, 6.0, ((0, 8),)),
        "values": centred(arg_keys[4], (TOKENS, HEAD), 1.0, 6.0, ((0, 8),)),
        "log_sums": jnp.clip(1.0 + 2.0 * jax.random.uniform(arg_keys[5], (HQ, TOKENS), jnp.float32) ** level_of(arg_keys[5], (HQ, TOKENS), ((0, 4), (1, 8)), -0.2, 0.2), 1.0, 3.0),
        "segment_ids": draw_segment_ids(jax.random.fold_in(arg_keys[11], 71), 0),
        "w_out": centred(arg_keys[7], (D, HQ * HEAD), D ** -0.5, 0.0625, ((0, 8), (1, 4))),
        "w_query": centred(arg_keys[8], (HQ * HEAD, D), (HQ * HEAD) ** -0.5, 0.1875, ((0, 4), (1, 8))),
        "w_key": centred(arg_keys[9], (HEAD, D), HEAD ** -0.5, 0.5),
        "w_value": centred(arg_keys[10], (HEAD, D), HEAD ** -0.5, 0.5),
    }


def to_natural(stored):
    width = stored.shape[1]
    blocks = stored.reshape(N_CONTEXT, 2, SPAN, width)
    return jnp.concatenate([blocks[:, 0], blocks[::-1, 1]], axis=0).reshape(LENGTH, width)

def to_stored(natural):
    width = natural.shape[1]
    blocks = natural.reshape(2 * N_CONTEXT, SPAN, width)
    return jnp.stack([blocks[:N_CONTEXT], blocks[N_CONTEXT:][::-1]], axis=1).reshape(LENGTH, width)

def sequence_grads(query_nat, dout_nat, lse_nat, delta_nat, key_nat, value_nat, seg_nat):
    inv_root = 1.0 / math.sqrt(HEAD)
    pad_keys = jnp.concatenate([jnp.zeros((SPAN, HEAD), key_nat.dtype), key_nat], axis=0)
    pad_values = jnp.concatenate([jnp.zeros((SPAN, HEAD), value_nat.dtype), value_nat], axis=0)
    pad_seg = jnp.concatenate([jnp.full((SPAN,), -1, jnp.int32), seg_nat.astype(jnp.int32)], axis=0)
    offsets = jnp.arange(SPAN, dtype=jnp.int32)
    key_offsets = jnp.arange(2 * SPAN, dtype=jnp.int32)

    def span_step(carry_acc, span_idx):
        key_acc, value_acc = carry_acc
        qstart = (span_idx * SPAN).astype(jnp.int32)
        query_blk = lax.dynamic_slice_in_dim(query_nat, qstart, SPAN, 0).astype(jnp.float32)
        dout_blk = lax.dynamic_slice_in_dim(dout_nat, qstart, SPAN, 0).astype(jnp.float32)
        lse_blk = lax.dynamic_slice_in_dim(lse_nat, qstart, SPAN, 1)
        delta_blk = lax.dynamic_slice_in_dim(delta_nat, qstart, SPAN, 1)
        key_blk = lax.dynamic_slice_in_dim(pad_keys, qstart, 2 * SPAN, 0).astype(jnp.float32)
        value_blk = lax.dynamic_slice_in_dim(pad_values, qstart, 2 * SPAN, 0).astype(jnp.float32)
        query_pos = qstart + offsets
        key_pos = qstart - SPAN + key_offsets
        seg_query = lax.dynamic_slice_in_dim(seg_nat.astype(jnp.int32), qstart, SPAN, 0)
        seg_key = lax.dynamic_slice_in_dim(pad_seg, qstart, 2 * SPAN, 0)
        allowed = (key_pos[None, :] <= query_pos[:, None]) & (key_pos[None, :] >= 0) & (seg_key[None, :] == seg_query[:, None])
        scores = jnp.einsum('qhe,ke->hqk', query_blk, key_blk) * inv_root
        prob_full = jnp.where(allowed[None], jnp.exp(scores - lse_blk[:, :, None]), 0.0)
        prob_low = lax.optimization_barrier(prob_full.astype(jnp.bfloat16)).astype(jnp.float32)
        dprobs = jnp.einsum('qhe,ke->hqk', dout_blk, value_blk)
        dscores = (prob_full * (dprobs - delta_blk[:, :, None])).astype(jnp.bfloat16)
        dscores = lax.optimization_barrier(dscores).astype(jnp.float32)
        dquery = (jnp.einsum('hqk,ke->qhe', dscores, key_blk) * inv_root).astype(jnp.bfloat16)
        key_heads = jnp.einsum('hqk,qhe->hke', dscores, query_blk) * inv_root
        value_heads = jnp.einsum('hqk,qhe->hke', prob_low, dout_blk)
        key_groups = key_heads.reshape(N_TENSOR, HQ // N_TENSOR, 2 * SPAN, HEAD).sum(axis=1)
        value_groups = value_heads.reshape(N_TENSOR, HQ // N_TENSOR, 2 * SPAN, HEAD).sum(axis=1)
        old_keys = lax.dynamic_slice_in_dim(key_acc, qstart, 2 * SPAN, 1)
        old_values = lax.dynamic_slice_in_dim(value_acc, qstart, 2 * SPAN, 1)
        key_acc = lax.dynamic_update_slice_in_dim(key_acc, old_keys + key_groups, qstart, 1)
        value_acc = lax.dynamic_update_slice_in_dim(value_acc, old_values + value_groups, qstart, 1)
        return ((key_acc, value_acc), dquery)
    zero_acc = jnp.zeros((N_TENSOR, LENGTH + SPAN, HEAD), jnp.float32)
    (key_acc, value_acc), dquery_blocks = lax.scan(span_step, (zero_acc, zero_acc), jnp.arange(2 * N_CONTEXT, dtype=jnp.int32))
    return (dquery_blocks.reshape(LENGTH, HQ * HEAD), key_acc[:, SPAN:], value_acc[:, SPAN:])

def reference(grad_out, queries, attended, keys, values, log_sums, segment_ids, w_out, w_query, w_key, w_value):
    group_cols = HQ // N_TENSOR * HEAD
    attn_grads = jnp.dot(grad_out, w_out, preferred_element_type=jnp.float32).astype(jnp.bfloat16)
    out_proj_grad = lax.dot_general(grad_out, attended, (((0,), (0,)), ((), ())), preferred_element_type=jnp.float32)
    row_delta = (attn_grads.astype(jnp.float32) * attended.astype(jnp.float32)).reshape(TOKENS, HQ, HEAD).sum(axis=2)
    results = []
    for seq_idx in range(SEQS):
        lower = seq_idx * LENGTH
        upper = lower + LENGTH
        query_nat = to_natural(queries[lower:upper]).reshape(LENGTH, HQ, HEAD)
        dout_nat = to_natural(attn_grads[lower:upper]).reshape(LENGTH, HQ, HEAD)
        lse_nat = to_natural(log_sums[:, lower:upper].T).T
        delta_nat = to_natural(row_delta[lower:upper]).T
        key_nat = to_natural(keys[lower:upper])
        value_nat = to_natural(values[lower:upper])
        dquery_nat, dkey_nat, dvalue_nat = sequence_grads(query_nat, dout_nat, lse_nat, delta_nat, key_nat, value_nat, segment_ids[seq_idx])
        dquery = to_stored(dquery_nat)
        summed = jnp.zeros((LENGTH, D), jnp.float32)
        for group in range(N_TENSOR):
            key_part = to_stored(dkey_nat[group].astype(jnp.bfloat16))
            value_part = to_stored(dvalue_nat[group].astype(jnp.bfloat16))
            cols = dquery[:, group * group_cols:(group + 1) * group_cols]
            part = jnp.dot(cols, w_query[group * group_cols:(group + 1) * group_cols], preferred_element_type=jnp.float32)
            part = part + jnp.dot(key_part, w_key, preferred_element_type=jnp.float32)
            part = part + jnp.dot(value_part, w_value, preferred_element_type=jnp.float32)
            summed = summed + lax.optimization_barrier(part.astype(jnp.bfloat16)).astype(jnp.float32)
        results.append(summed.astype(jnp.bfloat16))
    grad_input = jnp.concatenate(results, axis=0)
    return (grad_input, out_proj_grad)
```

```python
import functools
import math

import jax
import jax.numpy as jnp
from jax import lax
from jax.experimental import pallas as pl
from jax.experimental.pallas import tpu as pltpu
from jax.sharding import PartitionSpec as P

PLANE = ("dp", "context")
BF16 = jnp.bfloat16
F32 = jnp.float32


def swapped(x, axes, bit):
    size = lax.axis_size(axes)
    return lax.ppermute(x, axes, [(i, i ^ bit) for i in range(size)])


def neighbours(to_left, to_right):
    size, rank = lax.axis_size("context"), lax.axis_index("context")
    if size == 2:
        got = swapped(jnp.where(rank == 0, to_right, to_left), "context", 1)
        none = jnp.zeros_like(got)
        return jnp.where(rank == 0, none, got), jnp.where(rank == 0, got, none)
    up = [(i, i + 1) for i in range(size - 1)]
    down = [(i + 1, i) for i in range(size - 1)]
    return lax.ppermute(to_right, "context", up), lax.ppermute(to_left, "context", down)


def plane_bits():
    low, size = lax.axis_size("context"), lax.axis_size(PLANE)
    bits = [1 << i for i in range(size.bit_length() - 1)]
    return [low] + [b for b in reversed(bits) if b != low]


def plane_order():
    order = [0]
    for bit in reversed(plane_bits()):
        order = order + [k ^ bit for k in order]
    return order


def plane_exchange(blocks):
    order = plane_order()
    if len(order) <= 8:
        return [b if k == 0 else swapped(b, PLANE, k) for k, b in zip(order, blocks)]
    rank = lax.axis_index(PLANE)
    places = jnp.array(order, jnp.int32)
    inverse = jnp.argsort(places)
    stacked = jnp.stack(blocks)[inverse[jnp.arange(len(order)) ^ rank]]
    got = lax.all_to_all(stacked, PLANE, 0, 0, tiled=True)[places ^ rank]
    return [got[p] for p in range(len(order))]


def halves_orders(bits):
    return [bits[1:], bits[:0:-1]]


def plane_sum(parts, rows):
    bits, order = plane_bits(), plane_order()
    half = parts.shape[0] // 2
    got = swapped(parts[half:].astype(BF16), PLANE, bits[0])
    parts = parts[:half] + got.astype(F32)
    columns = parts.shape[1] // 2
    sums = []
    for side, path in enumerate(halves_orders(bits)):
        now = {
            k: parts[p * rows : (p + 1) * rows, side * columns : (side + 1) * columns]
            for p, k in enumerate(order[: len(order) // 2])
        }
        for bit in path:
            away = [k for k in now if k & bit]
            got = swapped(
                jnp.concatenate([now[k].astype(BF16) for k in away], axis=0), PLANE, bit
            )
            for i, k in enumerate(away):
                now[k ^ bit] = now[k ^ bit] + got[i * rows : (i + 1) * rows].astype(F32)
                del now[k]
        sums.append(now[0])
    return jnp.concatenate(sums, axis=1)


def plane_gather(x):
    bits, order = plane_bits(), plane_order()
    columns = x.shape[1] // 2
    sides = []
    for side, path in enumerate(halves_orders(bits)):
        held = {0: x[:, side * columns : (side + 1) * columns]}
        for bit in path:
            keys = list(held)
            got = swapped(jnp.concatenate([held[k] for k in keys], axis=0), PLANE, bit)
            for i, k in enumerate(keys):
                held[k ^ bit] = got[i * x.shape[0] : (i + 1) * x.shape[0]]
        sides.append(
            jnp.concatenate([held[k] for k in order[: len(order) // 2]], axis=0)
        )
    first = jnp.concatenate(sides, axis=1)
    return first, swapped(first, PLANE, bits[0])


def attention_kernel(
    tensor_ref, seg_query_ref, seg_key_ref, query_ref, dout_ref, attended_ref, kv_ref, log_ref,
    dquery_ref, kv_grads_ref, *, head_dim, peers,
):
    rank = tensor_ref[0]
    span = query_ref.shape[0] // 2
    heads = query_ref.shape[1] // head_dim
    sub = 2 * span // peers
    inv_root = 1.0 / math.sqrt(head_dim)

    def place(a):
        return pl.ds(pl.multiple_of(lax.bitwise_xor(rank, a) * sub, sub), sub)

    def by_head(x):
        return jnp.concatenate(
            [x[:, h * head_dim : (h + 1) * head_dim] for h in range(heads)], axis=0
        )

    def contract(x, y, dims):
        return lax.dot_general(x, y, (dims, ((), ())), preferred_element_type=F32)

    for b in range(2):
        rows = slice(b * span, (b + 1) * span)
        subs = range(b * peers // 2, (b + 1) * peers // 2)
        query = by_head(query_ref[rows, :])
        dout = by_head(jnp.concatenate([dout_ref[place(a), :] for a in subs], axis=0))
        attended = by_head(attended_ref[rows, :])
        key = kv_ref[b, :, :head_dim]
        value = kv_ref[b, :, head_dim:]
        log_rows = jnp.concatenate([log_ref[rows, h : h + 1] for h in range(heads)], axis=0)
        query_at = lax.broadcasted_iota(jnp.int32, (span, 2 * span), 0)
        key_at = lax.broadcasted_iota(jnp.int32, (span, 2 * span), 1) - span
        allowed = (key_at <= query_at) & (seg_query_ref[rows, :] == seg_key_ref[b : b + 1, :])
        allowed = jnp.concatenate([allowed] * heads, axis=0)
        scores = contract(query, key, ((1,), (1,))) * inv_root
        prob = jnp.where(allowed, jnp.exp(scores - log_rows), 0.0)
        delta = jnp.sum(
            dout.astype(F32) * attended.astype(F32), axis=1, keepdims=True
        )
        dprob = contract(dout, value, ((1,), (1,)))
        dscore = (prob * (dprob - delta)).astype(BF16)
        dquery = (contract(dscore, key, ((1,), (0,))) * inv_root).astype(BF16)
        for i, a in enumerate(subs):
            for h in range(heads):
                dquery_ref[place(a), h * head_dim : (h + 1) * head_dim] = dquery[
                    h * span + i * sub : h * span + (i + 1) * sub
                ]
        kv_grads_ref[b, :, :head_dim] = contract(dscore, query, ((0,), (0,))) * inv_root
        kv_grads_ref[b, :, head_dim:] = contract(prob.astype(BF16), dout, ((0,), (0,)))


def attention(rank, seg_query, seg_key, queries, dout, attended, kv, log_sums, head_dim, peers):
    vmem = pl.BlockSpec(memory_space=pltpu.VMEM)
    span = queries.shape[0] // 2
    heads = queries.shape[1] // head_dim
    pairs = 2 * heads * span * 2 * span
    return pl.pallas_call(
        functools.partial(attention_kernel, head_dim=head_dim, peers=peers),
        out_shape=(
            jax.ShapeDtypeStruct(queries.shape, BF16),
            jax.ShapeDtypeStruct(kv.shape, F32),
        ),
        in_specs=[pl.BlockSpec(memory_space=pltpu.SMEM)] + [vmem] * 7,
        out_specs=(vmem, vmem),
        compiler_params=pltpu.CompilerParams(vmem_limit_bytes=32 * 2**20),
        cost_estimate=pl.CostEstimate(
            flops=10 * pairs * head_dim, bytes_accessed=3 * 2**20, transcendentals=pairs
        ),
        name="attention",
    )(rank, seg_query, seg_key, queries, dout, attended, kv, log_sums)


def on_device(
    grad_out, queries, attended, keys, values, log_sums, segment_ids, w_out, w_query, w_key, w_value
):
    peers = lax.axis_size("tensor")
    tensor_rank = lax.axis_index("tensor")
    plane_rank = lax.axis_index(PLANE)
    cycle_size, cycle_pos = lax.axis_size("context"), lax.axis_index("context")
    last_rank = cycle_pos == cycle_size - 1
    own_rows, features = grad_out.shape
    width = w_out.shape[0]
    cols = queries.shape[1]
    span = queries.shape[0] // 2
    head_dim = keys.shape[1]
    order = plane_order()

    def own_block(x, rank, size, axis):
        return lax.dynamic_slice_in_dim(x, rank * size, size, axis=axis)

    w_out_all = [w_out] + [swapped(w_out, "tensor", j) for j in range(1, peers)]
    tokens = plane_exchange([own_block(grad_out, plane_rank ^ k, width, 1) for k in order])
    tokens = jnp.concatenate(tokens, axis=0)

    kv_pair = jnp.concatenate([keys, values], axis=1)
    own_low, own_high = kv_pair[:span], kv_pair[span:]
    left_low, right_high = neighbours(own_high, own_low)
    kv = jnp.stack(
        [
            jnp.concatenate([left_low, own_low], axis=0),
            jnp.concatenate([jnp.where(last_rank, own_low, right_high), own_high], axis=0),
        ]
    )
    seg_row = segment_ids[0]
    high_span = 2 * cycle_size - 1 - cycle_pos

    def seg_slice(at):
        return lax.dynamic_slice_in_dim(seg_row, jnp.maximum(at, 0) * span, span)

    seg_low, seg_high = seg_slice(cycle_pos), seg_slice(high_span)
    seg_before = jnp.where(cycle_pos == 0, -1, seg_slice(cycle_pos - 1))
    seg_query = jnp.concatenate([seg_low, seg_high])[:, None]
    seg_key = jnp.stack(
        [
            jnp.concatenate([seg_before, seg_low]),
            jnp.concatenate([seg_slice(high_span - 1), seg_high]),
        ]
    )
    log_rows = log_sums.T

    partial_attn = jnp.dot(
        tokens, jnp.concatenate(w_out_all, axis=1), preferred_element_type=F32
    )
    attn_own = plane_sum(partial_attn, own_rows).astype(BF16)
    dout = jnp.concatenate(
        [attn_own[:, :cols]]
        + [swapped(attn_own[:, j * cols : (j + 1) * cols], "tensor", j) for j in range(1, peers)],
        axis=0,
    )
    dquery, kv_grads = attention(
        tensor_rank.reshape(1), seg_query, seg_key, queries, dout, attended, kv, log_rows,
        head_dim, peers,
    )

    before_low, before_high = kv_grads[0, :span], kv_grads[1, :span]
    from_left, from_right = neighbours(
        before_low.astype(BF16), jnp.where(last_rank, 0.0, before_high).astype(BF16)
    )
    low = kv_grads[0, span:] + jnp.where(last_rank, before_high, 0.0) + from_right.astype(F32)
    high = kv_grads[1, span:] + from_left.astype(F32)
    kv_grads = jnp.concatenate([low, high], axis=0).astype(BF16)

    sent = [
        jnp.concatenate(
            [
                dquery[j * own_rows : (j + 1) * own_rows],
                own_block(kv_grads, tensor_rank ^ j, own_rows, 0),
            ],
            axis=1,
        )
        for j in range(peers)
    ]
    got = [sent[0]] + [swapped(sent[j], "tensor", j) for j in range(1, peers)]
    kv_own = sum(g[:, cols:].astype(F32) for g in got).astype(BF16)
    inner_own = jnp.concatenate([g[:, :cols] for g in got] + [kv_own], axis=1)
    inner = plane_gather(inner_own)
    w_in = jnp.concatenate(
        [w_query]
        + [swapped(w_query, "tensor", j) for j in range(1, peers)]
        + [own_block(w_key, plane_rank, width, 1), own_block(w_value, plane_rank, width, 1)],
        axis=0,
    )
    grads = [jnp.dot(x, w_in, preferred_element_type=F32).astype(BF16) for x in inner]
    blocks = [g[i * own_rows : (i + 1) * own_rows] for g in grads for i in range(len(order) // 2)]
    blocks = plane_exchange(blocks)
    grad_input = jnp.zeros((own_rows, features), BF16)
    for k, block in zip(order, blocks):
        grad_input = lax.dynamic_update_slice_in_dim(
            grad_input, block, (plane_rank ^ k) * width, axis=1
        )

    attended_own = [own_block(attended, tensor_rank ^ j, own_rows, 0) for j in range(peers)]
    attended_own = jnp.concatenate(
        [attended_own[0]] + [swapped(attended_own[j], "tensor", j) for j in range(1, peers)],
        axis=1,
    )
    attended_all = jnp.concatenate(plane_gather(attended_own), axis=0)
    partial_out = lax.dot_general(
        tokens, attended_all, (((0,), (0,)), ((), ())), preferred_element_type=F32
    )
    out_proj_grad = partial_out[:, :cols]
    for j in range(1, peers):
        out_proj_grad = out_proj_grad + swapped(
            partial_out[:, j * cols : (j + 1) * cols].astype(BF16), "tensor", j
        ).astype(F32)
    return (grad_input, out_proj_grad)


def solution(mesh):
    placed = (
        P(("dp", "context", "tensor"), None),
        P(("dp", "context"), "tensor"),
        P(("dp", "context"), "tensor"),
        P(("dp", "context"), None),
        P(("dp", "context"), None),
        P("tensor", ("dp", "context")),
        P("dp", None),
        P(("dp", "context"), "tensor"),
        P("tensor", ("dp", "context")),
        P(),
        P(),
    )
    return jax.shard_map(
        on_device,
        mesh=mesh,
        in_specs=placed,
        out_specs=(P(("dp", "context", "tensor"), None), P(("dp", "context"), "tensor")),
        check_vma=False,
    )
```

```python
import functools
import math

import jax
import jax.numpy as jnp
from jax import lax
from jax.experimental import pallas as pl
from jax.experimental.pallas import tpu as pltpu
from jax.sharding import PartitionSpec as P

PLANE = ("dp", "context")
BF16 = jnp.bfloat16
F32 = jnp.float32
TENSOR_ORDER = (0, 2, 1, 3)


def swapped(x, axes, bit):
    size = lax.axis_size(axes)
    return lax.ppermute(x, axes, [(i, i ^ bit) for i in range(size)])


def neighbours(to_left, to_right):
    size = lax.axis_size("context")
    up = [(i, i + 1) for i in range(size - 1)]
    down = [(i + 1, i) for i in range(size - 1)]
    return [lax.ppermute(to_right, "context", up), lax.ppermute(to_left, "context", down)]


def contract(x, y, dims):
    return lax.dot_general(x, y, (dims, ((), ())), preferred_element_type=F32)


VMEM = pl.BlockSpec(memory_space=pltpu.VMEM)
ANY = pl.BlockSpec(memory_space=pl.ANY)
SMALL = pl.CostEstimate(flops=0, bytes_accessed=0, transcendentals=0)


def cut_kernel(
    ranks_ref, x_ref, weight_ref, att_ref, *refs, parts, pair
):
    out_refs, (to_2_ref, to_1_ref, att_own_ref) = refs[:-3], refs[-3:]
    width = out_refs[0].shape[1] // 2
    for i, k in enumerate(parts):
        for half in range(2):
            owner = lax.bitwise_xor(ranks_ref[0], k ^ (half * pair))
            start = pl.multiple_of(owner * width, width)
            out_refs[i][:, half * width : (half + 1) * width] = x_ref[:, pl.ds(start, width)]
    rows, depth = att_own_ref.shape[0], weight_ref.shape[0]

    def att_of(j):
        owner = lax.bitwise_xor(ranks_ref[1], j)
        return att_ref[pl.ds(pl.multiple_of(owner * rows, rows), rows), :]

    att_own_ref[...] = att_of(0)
    to_2_ref[:rows, :] = att_of(2)
    to_2_ref[rows : rows + depth, :] = weight_ref[...]
    to_2_ref[rows + depth :, :] = att_of(3)
    to_1_ref[:depth, :] = weight_ref[...]
    to_1_ref[depth:, :] = att_of(1)


def cut(ranks, x, weight, att, parts, pair):
    rows, (depth, cols) = x.shape[0], weight.shape
    return pl.pallas_call(
        functools.partial(cut_kernel, parts=parts, pair=pair),
        out_shape=[jax.ShapeDtypeStruct((rows, 2 * depth), x.dtype) for _ in parts]
        + [
            jax.ShapeDtypeStruct((depth + 2 * rows, cols), x.dtype),
            jax.ShapeDtypeStruct((depth + rows, cols), x.dtype),
            jax.ShapeDtypeStruct((rows, cols), x.dtype),
        ],
        in_specs=[pl.BlockSpec(memory_space=pltpu.SMEM)] + [VMEM] * 3,
        out_specs=[VMEM] * (len(parts) + 3),
        compiler_params=pltpu.CompilerParams(vmem_limit_bytes=40 * 2**20),
        cost_estimate=SMALL,
        name="cut",
    )(ranks, x, weight, att)


def project_kernel(*refs, tokens, starts, width):
    pieces = len(starts)
    att_ref, token_refs, refs = refs[0], refs[1 : 1 + tokens], refs[1 + tokens :]
    own_refs, pair_refs = refs[:pieces], refs[pieces : 2 * pieces]
    out_refs, att_out_ref, held = refs[-2 - tokens : -2], refs[-2], refs[-1]
    rows = token_refs[0].shape[0]
    cols = own_refs[0].shape[1]
    for i, ref in enumerate(token_refs):
        held[i * rows : (i + 1) * rows, :] = ref[...]
    for j, start in enumerate(starts):
        at, used = slice(j * cols, (j + 1) * cols), slice(start, start + width)
        total = contract(held[:, :width], own_refs[j][used, :], ((1,), (0,)))
        total = total + contract(held[:, width:], pair_refs[j][used, :], ((1,), (0,)))
        for i, ref in enumerate(out_refs):
            ref[:, at] = total[i * rows : (i + 1) * rows].astype(ref.dtype)
        if j == 0:
            att_out_ref[:, at] = att_ref[...]
        else:
            beside = 0 if start else width
            att_out_ref[:, at] = own_refs[j][beside : beside + rows, :]


def project(att, tokens, own, pair, starts, width, behind):
    rows, cols = att.shape
    columns = len(own) * cols
    return pl.pallas_call(
        functools.partial(project_kernel, tokens=len(tokens), starts=starts, width=width),
        out_shape=[
            jax.ShapeDtypeStruct((rows, columns), BF16 if i else F32) for i in range(len(tokens))
        ]
        + [jax.ShapeDtypeStruct((rows, columns), BF16)],
        in_specs=[VMEM] * (1 + len(tokens) + 2 * len(own)) + [ANY] * len(behind),
        out_specs=[VMEM] * (len(tokens) + 1),
        scratch_shapes=[pltpu.VMEM((rows * len(tokens), 2 * width), BF16)],
        compiler_params=pltpu.CompilerParams(vmem_limit_bytes=40 * 2**20),
        cost_estimate=SMALL,
        name="project",
    )(att, *tokens, *own, *pair, *behind)


def hand_on_kernel(x_ref, *refs):
    refs[-1][...] = x_ref[-refs[-1].shape[0] :, :]


def hand_on(x, rows, behind):
    return pl.pallas_call(
        hand_on_kernel,
        out_shape=jax.ShapeDtypeStruct((rows, x.shape[1]), x.dtype),
        in_specs=[VMEM] + [ANY] * len(behind),
        out_specs=VMEM,
        compiler_params=pltpu.CompilerParams(vmem_limit_bytes=40 * 2**20),
        cost_estimate=SMALL,
        name="hand_on",
    )(x, *behind)


def add_kernel(own_ref, *refs, parts, pieces):
    part_refs, out_refs = refs[:parts], refs[parts:]
    cols = out_refs[0].shape[1]
    total = own_ref[...]
    for ref in part_refs:
        total = total + ref[...].astype(F32)
    for j, ref in enumerate(out_refs):
        ref[...] = total[:, j * cols : (j + 1) * cols].astype(BF16)


def add_up(own, parts, pieces):
    rows, columns = own.shape
    return pl.pallas_call(
        functools.partial(add_kernel, parts=len(parts), pieces=pieces),
        out_shape=[jax.ShapeDtypeStruct((rows, columns // pieces), BF16)] * pieces,
        in_specs=[VMEM] * (1 + len(parts)),
        out_specs=[VMEM] * pieces,
        compiler_params=pltpu.CompilerParams(vmem_limit_bytes=60 * 2**20),
        cost_estimate=SMALL,
        name="add_up",
    )(own, *parts)


def join_kernel(ranks_ref, kv_ref, *refs, pieces, backs, later):
    refs = refs[later:]
    query_refs, back_refs = refs[:pieces], refs[pieces : pieces + backs]
    (query_ref, away_ref, next_ref, own_ref), held = refs[pieces + backs :][:4], refs[-1]
    rows, cols = query_refs[0].shape
    span = kv_ref.shape[0] // 2
    for i, ref in enumerate(query_refs):
        query_ref[:, i * cols : (i + 1) * cols] = ref[...]
    held[...] = kv_ref[...]
    if backs == 1:
        at = pl.ds(pl.multiple_of(ranks_ref[2] * span, span), span)
        held[at, :] = held[at, :] + back_refs[0][...].astype(F32)
    else:
        held[span:, :] = held[span:, :] + back_refs[0][...].astype(F32)
        held[:span, :] = held[:span, :] + back_refs[1][...].astype(F32)

    def rank_rows(j):
        at = pl.ds(pl.multiple_of(lax.bitwise_xor(ranks_ref[1], j) * rows, rows), rows)
        return held[at, :]

    away_ref[:rows, :] = rank_rows(2).astype(BF16)
    away_ref[rows:, :] = rank_rows(3).astype(BF16)
    next_ref[...] = rank_rows(1)
    own_ref[...] = rank_rows(0)


def join(ranks, kv, back, queries, later):
    rows, cols = queries[0].shape
    width = kv.shape[1]
    return pl.pallas_call(
        functools.partial(
            join_kernel, pieces=len(queries), backs=len(back), later=len(later)
        ),
        out_shape=[
            jax.ShapeDtypeStruct((rows, cols * len(queries)), BF16),
            jax.ShapeDtypeStruct((2 * rows, width), BF16),
            jax.ShapeDtypeStruct((rows, width), F32),
            jax.ShapeDtypeStruct((rows, width), F32),
            *[jax.ShapeDtypeStruct(x.shape, x.dtype) for x in later],
        ],
        in_specs=[pl.BlockSpec(memory_space=pltpu.SMEM), VMEM]
        + [ANY] * len(later)
        + [VMEM] * (len(queries) + len(back)),
        out_specs=[VMEM] * 4 + [ANY] * len(later),
        scratch_shapes=[pltpu.VMEM(kv.shape, F32)],
        input_output_aliases={2 + i: 4 + i for i in range(len(later))},
        compiler_params=pltpu.CompilerParams(vmem_limit_bytes=60 * 2**20),
        cost_estimate=SMALL,
        name="join",
    )(ranks, kv, *later, *queries, *back)


def outer_kernel(*refs, tokens, atts, behind):
    (own_ref, pair_ref), (held, att_held) = refs[tokens + atts + behind :][:2], refs[-2:]
    for block_refs, whole in ((refs[:tokens], held), (refs[tokens : tokens + atts], att_held)):
        start = 0
        for ref in block_refs:
            whole[start : start + ref.shape[0], :] = ref[...]
            start += ref.shape[0]
    width = own_ref.shape[0]
    step = min(width, 256)
    for e in range(0, width, step):
        at = slice(e, e + step)
        own_ref[at, :] = contract(held[:, at], att_held[...], ((0,), (0,)))
        pair_at = slice(width + e, width + e + step)
        pair_ref[at, :] = contract(held[:, pair_at], att_held[...], ((0,), (0,))).astype(BF16)


def outer(tokens, atts, later, behind):
    width, columns = tokens[0].shape[1] // 2, atts[0].shape[1]
    depth = tokens[0].shape[0] * len(tokens)
    return pl.pallas_call(
        functools.partial(
            outer_kernel, tokens=len(tokens), atts=len(atts), behind=len(later) + len(behind)
        ),
        out_shape=[
            jax.ShapeDtypeStruct((width, columns), F32),
            jax.ShapeDtypeStruct((width, columns), BF16),
            *[jax.ShapeDtypeStruct(x.shape, x.dtype) for x in later],
        ],
        in_specs=[VMEM] * (len(tokens) + len(atts)) + [ANY] * (len(later) + len(behind)),
        out_specs=[VMEM] * 2 + [ANY] * len(later),
        input_output_aliases={len(tokens) + len(atts) + i: 2 + i for i in range(len(later))},
        scratch_shapes=[pltpu.VMEM((depth, 2 * width), BF16), pltpu.VMEM((depth, columns), BF16)],
        compiler_params=pltpu.CompilerParams(vmem_limit_bytes=40 * 2**20),
        cost_estimate=SMALL,
        name="outer",
    )(*tokens, *atts, *later, *behind)


def feed_kernel(*refs, tokens, sides):
    query_refs, kv_refs, refs = refs[:tokens], refs[tokens : 2 * tokens], refs[2 * tokens :]
    weights, refs = [refs[i * sides : (i + 1) * sides] for i in range(2)], refs[2 * sides :]
    w_kv_ref, out_refs, held = refs[0], refs[-1 - tokens : -1], refs[-1]
    rows, columns = query_refs[0].shape
    width = w_kv_ref.shape[1] // 2
    for i in range(tokens):
        held[i * rows : (i + 1) * rows, :columns] = query_refs[i][...]
        held[i * rows : (i + 1) * rows, columns:] = kv_refs[i][...]
    for half in range(2):
        at = slice(half * width, (half + 1) * width)
        total = contract(held[:, columns:], w_kv_ref[:, at], ((1,), (0,)))
        start = 0
        for w in weights[half]:
            depth = w.shape[0]
            total = total + contract(held[:, start : start + depth], w[...], ((1,), (0,)))
            start += depth
        for i, ref in enumerate(out_refs):
            ref[:, at] = total[i * rows : (i + 1) * rows].astype(BF16)


def feed(queries, kvs, own, pair, w_kv, behind):
    rows, columns = queries[0].shape
    width = w_kv.shape[1]
    depth = columns + w_kv.shape[0]
    return pl.pallas_call(
        functools.partial(feed_kernel, tokens=len(queries), sides=len(own)),
        out_shape=[jax.ShapeDtypeStruct((rows, width), BF16)] * len(queries),
        in_specs=[VMEM] * (2 * len(queries) + 2 * len(own) + 1) + [ANY] * len(behind),
        out_specs=[VMEM] * len(queries),
        scratch_shapes=[pltpu.VMEM((rows * len(queries), depth), BF16)],
        compiler_params=pltpu.CompilerParams(vmem_limit_bytes=60 * 2**20),
        cost_estimate=SMALL,
        name="feed",
    )(*queries, *kvs, *own, *pair, w_kv, *behind)


def attention_kernel(
    ranks_ref, seg_query_ref, seg_key_ref, query_ref, attended_ref, key_ref, value_ref, log_ref,
    *refs, peers, befores, cycle_size,
):
    dout_refs, before_refs = refs[:peers], refs[peers : peers + befores]
    dquery_refs, away_refs = refs[-3 - befores - peers : -3 - befores], refs[-3 - befores : -3]
    kv_grads_ref, dout_held, dquery_held = refs[-3:]
    rank, last_rank = ranks_ref[1], ranks_ref[2] == cycle_size - 1
    head_dim = key_ref.shape[1]
    span = query_ref.shape[0] // 2
    heads = query_ref.shape[1] // head_dim
    sub = 2 * span // peers
    inv_root = 1.0 / math.sqrt(head_dim)

    def place(a):
        return pl.ds(pl.multiple_of(a * sub, sub), sub)

    def by_head(x):
        return jnp.concatenate(
            [x[:, h * head_dim : (h + 1) * head_dim] for h in range(heads)], axis=0
        )

    for j, ref in zip(TENSOR_ORDER, dout_refs):
        dout_held[place(lax.bitwise_xor(rank, j)), :] = ref[...]
    before = []
    for b in range(2):
        rows = slice(b * span, (b + 1) * span)
        query = by_head(query_ref[rows, :])
        dout = by_head(dout_held[rows, :])
        attended = by_head(attended_ref[rows, :])
        key_before = before_refs[b % befores][:, :head_dim]
        value_before = before_refs[b % befores][:, head_dim:]
        if b == 1:
            key_before = jnp.where(last_rank, key_ref[:span, :], key_before)
            value_before = jnp.where(last_rank, value_ref[:span, :], value_before)
        key = jnp.concatenate([key_before, key_ref[rows, :]], axis=0)
        value = jnp.concatenate([value_before, value_ref[rows, :]], axis=0)
        log_rows = jnp.concatenate([log_ref[rows, h : h + 1] for h in range(heads)], axis=0)
        query_at = lax.broadcasted_iota(jnp.int32, (span, 2 * span), 0)
        key_at = lax.broadcasted_iota(jnp.int32, (span, 2 * span), 1) - span
        allowed = (key_at <= query_at) & (seg_query_ref[rows, :] == seg_key_ref[b : b + 1, :])
        allowed = jnp.concatenate([allowed] * heads, axis=0)
        scores = contract(query, key, ((1,), (1,))) * inv_root
        prob = jnp.where(allowed, jnp.exp(scores - log_rows), 0.0)
        delta = jnp.sum(dout.astype(F32) * attended.astype(F32), axis=1, keepdims=True)
        dprob = contract(dout, value, ((1,), (1,)))
        dscore = (prob * (dprob - delta)).astype(BF16)
        dquery = (contract(dscore, key, ((1,), (0,))) * inv_root).astype(BF16)
        for h in range(heads):
            dquery_held[rows, h * head_dim : (h + 1) * head_dim] = dquery[
                h * span : (h + 1) * span
            ]
        key_grads = contract(dscore, query, ((0,), (0,))) * inv_root
        value_grads = contract(prob.astype(BF16), dout, ((0,), (0,)))
        kv_grads_ref[rows, :head_dim] = key_grads[span:]
        kv_grads_ref[rows, head_dim:] = value_grads[span:]
        before.append((key_grads[:span], value_grads[:span]))
    for i, half in enumerate((slice(0, head_dim), slice(head_dim, 2 * head_dim))):
        low, high = before[0][i], before[1][i]
        kv_grads_ref[:span, half] = kv_grads_ref[:span, half] + jnp.where(last_rank, high, 0.0)
        if befores == 1:
            away_refs[0][:, half] = jnp.where(last_rank, low, high).astype(BF16)
        else:
            away_refs[0][:, half] = low.astype(BF16)
            away_refs[1][:, half] = jnp.where(last_rank, 0.0, high).astype(BF16)
    for j, ref in zip(TENSOR_ORDER, dquery_refs):
        ref[...] = dquery_held[place(lax.bitwise_xor(rank, j)), :]


def attention(
    ranks, seg_query, seg_key, queries, attended, keys, values, log_sums, dout, before, behind,
    cycle_size,
):
    kv_shape = (keys.shape[0], 2 * keys.shape[1])
    return pl.pallas_call(
        functools.partial(
            attention_kernel, peers=len(dout), befores=len(before), cycle_size=cycle_size
        ),
        out_shape=[jax.ShapeDtypeStruct(x.shape, BF16) for x in (*dout, *before)]
        + [jax.ShapeDtypeStruct(kv_shape, F32)],
        in_specs=[pl.BlockSpec(memory_space=pltpu.SMEM)]
        + [VMEM] * (7 + len(dout) + len(before))
        + [ANY] * len(behind),
        out_specs=[VMEM] * (len(dout) + len(before) + 1),
        scratch_shapes=[pltpu.VMEM(queries.shape, BF16)] * 2,
        compiler_params=pltpu.CompilerParams(vmem_limit_bytes=32 * 2**20),
        cost_estimate=SMALL,
        name="attention",
    )(ranks, seg_query, seg_key, queries, attended, keys, values, log_sums, *dout, *before, *behind)


def on_device(
    grad_out, queries, attended, keys, values, log_sums, segment_ids, w_out, w_query, w_key, w_value
):
    tensor_rank = lax.axis_index("tensor")
    plane_rank = lax.axis_index(PLANE)
    cycle_size, cycle_pos = lax.axis_size("context"), lax.axis_index("context")
    own_rows, features = grad_out.shape
    width = w_out.shape[0]
    cols = queries.shape[1]
    span = queries.shape[0] // 2
    head_dim = keys.shape[1]
    pair = cycle_size
    bits = [1 << i for i in range(lax.axis_size(PLANE).bit_length() - 1)]
    bits = [bit for bit in reversed(bits) if bit != pair]
    meets = [0]
    for bit in bits:
        meets += [k ^ bit for k in meets]
    meets = meets[1:]

    def own_block(x, rank, size, axis):
        return lax.dynamic_slice_in_dim(x, rank * size, size, axis=axis)

    def pair_blocks(x, k):
        return jnp.concatenate(
            [own_block(x, plane_rank ^ k, width, 1), own_block(x, plane_rank ^ k ^ pair, width, 1)],
            axis=1,
        )

    def plane_gather(x):
        return [x] + [swapped(x, PLANE, k) for k in meets]

    def along(x, j):
        return swapped(x, "tensor", j)

    ranks = jnp.stack([plane_rank, tensor_rank, cycle_pos])
    *tokens, to_2, to_1, att_own = cut(ranks, grad_out, w_out, attended, [0] + meets, pair)
    out_2, out_1 = along(to_2, 2), along(to_1, 1)
    tokens = tokens[:1] + [swapped(x, PLANE, k) for k, x in zip(meets, tokens[1:])]
    out_3 = along(hand_on(out_2, width + own_rows, tokens[1:]), 1)
    w_out_own = [w_out, out_2, out_1, out_3]
    w_out_pair = [swapped(w, PLANE, pair) for w in w_out_own]
    starts = (0, own_rows, 0, 0)

    query_2, query_1 = along(w_query, 2), along(w_query, 1)

    kv_pair = jnp.concatenate([keys, values], axis=1)
    if cycle_size == 2:
        before = [swapped(own_block(kv_pair, cycle_pos, span, 0), "context", 1)]
    else:
        before = neighbours(kv_pair[span:], kv_pair[:span])
    seg_row = segment_ids[0]
    high_span = 2 * cycle_size - 1 - cycle_pos

    def seg_slice(at):
        return lax.dynamic_slice_in_dim(seg_row, jnp.maximum(at, 0) * span, span)

    seg_low, seg_high = seg_slice(cycle_pos), seg_slice(high_span)
    seg_before = jnp.where(cycle_pos == 0, -1, seg_slice(cycle_pos - 1))
    seg_query = jnp.concatenate([seg_low, seg_high])[:, None]
    seg_key = jnp.stack(
        [
            jnp.concatenate([seg_before, seg_low]),
            jnp.concatenate([seg_slice(high_span - 1), seg_high]),
        ]
    )
    log_rows = log_sums.T

    *partial_attn, att_own = project(
        att_own, tokens, w_out_own, w_out_pair, starts, width, before
    )
    parts = [swapped(x, PLANE, k) for k, x in zip(meets, partial_attn[1:])]
    attn_own = list(add_up(partial_attn[0], parts, 4))
    dout = attn_own[:1] + [along(x, j) for x, j in zip(attn_own[1:], TENSOR_ORDER[1:])]
    *dquery, kv_grads = attention(
        ranks, seg_query, seg_key, queries, attended, keys, values, log_rows, dout, before,
        [query_2, query_1], cycle_size,
    )
    dquery, away = dquery[:4], dquery[4:]

    atts = [att_own]
    for bit in bits:
        atts.append(swapped(jnp.concatenate(atts, axis=0), PLANE, bit))

    dquery = dquery[:1] + [along(x, j) for x, j in zip(dquery[1:], TENSOR_ORDER[1:])]
    back = [swapped(away[0], "context", 1)] if cycle_size == 2 else neighbours(*away)
    dquery_own, kv_away, kv_next, kv_rest, query_2, query_1 = join(
        ranks, kv_grads, back, dquery, [query_2, query_1]
    )
    dquery_met = plane_gather(dquery_own)
    got = along(kv_away, 2)
    kv_next = along((kv_next + got[own_rows:].astype(F32)).astype(BF16), 1)
    kv_own = (kv_rest + got[:own_rows].astype(F32) + kv_next.astype(F32)).astype(BF16)
    kv_met = plane_gather(kv_own)

    query_3 = along(query_2, 1)

    out_own, out_pair, *w_query_own = outer(
        tokens, atts, [query_2, query_1, query_3], [dquery_met[1], got]
    )
    w_query_own = [w_query, *w_query_own]
    w_query_pair = [swapped(w, PLANE, pair) for w in w_query_own]
    got = swapped(out_pair, PLANE, pair)

    def out_block(i):
        at = slice(i * cols, (i + 1) * cols)
        return out_own[:, at] + got[:, at].astype(F32)

    to_3 = out_block(3).astype(BF16)
    from_3 = along(to_3, 1)
    from_1 = along(out_block(2).astype(BF16), 1)
    from_2 = along((out_block(1) + from_3.astype(F32)).astype(BF16), 2)
    out_proj_grad = out_block(0) + from_1.astype(F32) + from_2.astype(F32)

    w_kv = jnp.concatenate([pair_blocks(w_key, 0), pair_blocks(w_value, 0)], axis=0)
    blocks = feed(dquery_met, kv_met, w_query_own, w_query_pair, w_kv, [to_3])
    blocks = [(0, blocks[0])] + [(k, swapped(x, PLANE, k)) for k, x in zip(meets, blocks[1:])]
    grad_input = jnp.zeros((own_rows, features), BF16)
    for k, block in blocks:
        for i, owner in enumerate((plane_rank ^ k, plane_rank ^ k ^ pair)):
            grad_input = lax.dynamic_update_slice_in_dim(
                grad_input, block[:, i * width : (i + 1) * width], owner * width, axis=1
            )
    return (grad_input, out_proj_grad)


def solution(mesh):
    placed = (
        P(("dp", "context", "tensor"), None),
        P(("dp", "context"), "tensor"),
        P(("dp", "context"), "tensor"),
        P(("dp", "context"), None),
        P(("dp", "context"), None),
        P("tensor", ("dp", "context")),
        P("dp", None),
        P(("dp", "context"), "tensor"),
        P("tensor", ("dp", "context")),
        P(),
        P(),
    )
    return jax.shard_map(
        on_device,
        mesh=mesh,
        in_specs=placed,
        out_specs=(P(("dp", "context", "tensor"), None), P(("dp", "context"), "tensor")),
        check_vma=False,
    )
```

```python
import functools
import math

import jax
import jax.numpy as jnp
from jax import lax
from jax.experimental import pallas as pl
from jax.experimental.pallas import tpu as pltpu
from jax.sharding import PartitionSpec as P

PLANE = ("dp", "context")
BF16 = jnp.bfloat16
F32 = jnp.float32
TENSOR_ORDER = (0, 2, 1, 3)


def swapped(x, axes, bit, name):
    size = lax.axis_size(axes)
    with jax.named_scope(name):
        return lax.ppermute(x, axes, [(i, i ^ bit) for i in range(size)])


def neighbours(to_left, to_right):
    size = lax.axis_size("context")
    up = [(i, i + 1) for i in range(size - 1)]
    down = [(i + 1, i) for i in range(size - 1)]
    return [lax.ppermute(to_right, "context", up), lax.ppermute(to_left, "context", down)]


def contract(x, y, dims):
    return lax.dot_general(x, y, (dims, ((), ())), preferred_element_type=F32)


VMEM = pl.BlockSpec(memory_space=pltpu.VMEM)
ANY = pl.BlockSpec(memory_space=pl.ANY)
FLOPS = 4 * 10**10
SMALL = pl.CostEstimate(flops=0, bytes_accessed=0, transcendentals=0)


def cut_kernel(ranks_ref, x_ref, key_ref, value_ref, *refs, parts, pair, width, carrier):
    out_refs, sems = refs[:-1], refs[-1]
    moves = []
    for i, k in enumerate(parts):
        for half in range(2):
            owner = lax.bitwise_xor(ranks_ref[0], k ^ (half * pair))
            start = pl.multiple_of(owner * width, width)
            moves.append(
                (x_ref.at[:, pl.ds(start, width)], out_refs[i].at[:, half * width : (half + 1) * width])
            )
    if carrier is not None:
        rows, start = x_ref.shape[0], 2 * width
        for half in range(2):
            at = pl.ds(pl.multiple_of((2 * ranks_ref[2] + half) * rows, rows), rows)
            for ref in (key_ref, value_ref):
                end = start + ref.shape[1]
                moves.append((ref.at[at, :], out_refs[carrier].at[:, start:end]))
                start = end
    copies = [pltpu.make_async_copy(x, y, sems.at[i]) for i, (x, y) in enumerate(moves)]
    for copy in copies:
        copy.start()
    for copy in copies:
        copy.wait()


def cut(ranks, x, keys, values, parts, pair, width, carrier):
    rows = x.shape[0]
    extra = 2 * (keys.shape[1] + values.shape[1])
    return pl.pallas_call(
        functools.partial(cut_kernel, parts=parts, pair=pair, width=width, carrier=carrier),
        out_shape=[
            jax.ShapeDtypeStruct((rows, 2 * width + (extra if i == carrier else 0)), x.dtype)
            for i in range(len(parts))
        ],
        in_specs=[pl.BlockSpec(memory_space=pltpu.SMEM)] + [ANY] * 3,
        out_specs=[VMEM] * len(parts),
        scratch_shapes=[pltpu.SemaphoreType.DMA((2 * len(parts) + 4,))],
        compiler_params=pltpu.CompilerParams(vmem_limit_bytes=60 * 2**20),
        cost_estimate=SMALL,
        name="cut",
    )(ranks, x, keys, values)


def project_kernel(*refs, tokens, pieces, carrier):
    token_refs, refs = refs[:tokens], refs[tokens:]
    own_refs, pair_refs, refs = refs[:pieces], refs[pieces : 2 * pieces], refs[2 * pieces :]
    out_refs, held = refs[:tokens], refs[-1]
    rows = token_refs[0].shape[0]
    width, cols = own_refs[0].shape
    for i, ref in enumerate(token_refs):
        held[i * rows : (i + 1) * rows, :] = ref[:, : 2 * width]
    if carrier is not None:
        before_ref = refs[tokens]
        depth = before_ref.shape[1]
        for half in range(2):
            start = 2 * width + half * depth
            before_ref[half * rows : (half + 1) * rows, :] = token_refs[carrier][
                :, start : start + depth
            ]
    for j in range(pieces):
        total = contract(held[:, :width], own_refs[j][...], ((1,), (0,)))
        total = total + contract(held[:, width:], pair_refs[j][...], ((1,), (0,)))
        for i, ref in enumerate(out_refs):
            ref[:, j * cols : (j + 1) * cols] = total[i * rows : (i + 1) * rows].astype(ref.dtype)


def project(tokens, own, pair, carrier):
    rows = tokens[0].shape[0]
    width, cols = own[0].shape
    out_shape = [
        jax.ShapeDtypeStruct((rows, len(own) * cols), BF16 if i else F32)
        for i in range(len(tokens))
    ]
    if carrier is not None:
        extra = (tokens[carrier].shape[1] - 2 * width) // 2
        out_shape.append(jax.ShapeDtypeStruct((2 * rows, extra), BF16))
    return pl.pallas_call(
        functools.partial(
            project_kernel, tokens=len(tokens), pieces=len(own), carrier=carrier
        ),
        out_shape=out_shape,
        in_specs=[VMEM] * (len(tokens) + 2 * len(own)),
        out_specs=[VMEM] * len(out_shape),
        scratch_shapes=[pltpu.VMEM((rows * len(tokens), 2 * width), BF16)],
        compiler_params=pltpu.CompilerParams(vmem_limit_bytes=60 * 2**20),
        cost_estimate=SMALL,
        name="project",
    )(*tokens, *own, *pair)


def hand_on_kernel(*refs):
    pass


def hand_on(arrays, behind, flops=0):
    return pl.pallas_call(
        hand_on_kernel,
        out_shape=[jax.ShapeDtypeStruct(x.shape, x.dtype) for x in arrays],
        in_specs=[ANY] * (len(arrays) + len(behind)),
        out_specs=[ANY] * len(arrays),
        input_output_aliases={i: i for i in range(len(arrays))},
        compiler_params=pltpu.CompilerParams(vmem_limit_bytes=16 * 2**20),
        cost_estimate=pl.CostEstimate(flops=flops, bytes_accessed=0, transcendentals=0),
        name="hand_on",
    )(*arrays, *behind)


def add_kernel(ranks_ref, own_ref, att_ref, *refs, parts):
    part_refs, out_refs = refs[:parts], refs[parts:]
    rows, cols = out_refs[0].shape
    total = own_ref[...]
    for ref in part_refs:
        total = total + ref[...].astype(F32)
    for j, (distance, ref) in enumerate(zip(TENSOR_ORDER, out_refs)):
        ref[:rows, :] = total[:, j * cols : (j + 1) * cols].astype(BF16)
        if distance:
            owner = lax.bitwise_xor(ranks_ref[1], distance)
            ref[rows:, :] = att_ref[pl.ds(pl.multiple_of(owner * rows, rows), rows), :]


def add_up(ranks, own, attended, parts):
    rows, cols = own.shape[0], attended.shape[1]
    return pl.pallas_call(
        functools.partial(add_kernel, parts=len(parts)),
        out_shape=[
            jax.ShapeDtypeStruct((2 * rows if j else rows, cols), BF16) for j in TENSOR_ORDER
        ],
        in_specs=[pl.BlockSpec(memory_space=pltpu.SMEM)] + [VMEM] * (2 + len(parts)),
        out_specs=[VMEM] * len(TENSOR_ORDER),
        compiler_params=pltpu.CompilerParams(vmem_limit_bytes=60 * 2**20),
        cost_estimate=SMALL,
        name="add_up",
    )(ranks, own, attended, *parts)


def join_kernel(ranks_ref, kv_ref, *refs, backs):
    back_refs, (away_ref, next_ref, own_ref), held = refs[:backs], refs[-5:-2], refs[-1]
    rows = own_ref.shape[0]
    span = kv_ref.shape[0] // 2
    held[...] = kv_ref[...]
    if backs == 1:
        at = pl.ds(pl.multiple_of(ranks_ref[2] * span, span), span)
        held[at, :] = held[at, :] + back_refs[0][...].astype(F32)
    else:
        held[span:, :] = held[span:, :] + back_refs[0][...].astype(F32)
        held[:span, :] = held[:span, :] + back_refs[1][...].astype(F32)

    def rank_rows(j):
        at = pl.ds(pl.multiple_of(lax.bitwise_xor(ranks_ref[1], j) * rows, rows), rows)
        return held[at, :]

    away_ref[:rows, :] = rank_rows(2).astype(BF16)
    away_ref[rows:, :] = rank_rows(3).astype(BF16)
    next_ref[...] = rank_rows(1)
    own_ref[...] = rank_rows(0)


def join(ranks, kv, back, behind, later):
    rows, width = kv.shape[0] // len(TENSOR_ORDER), kv.shape[1]
    return pl.pallas_call(
        functools.partial(join_kernel, backs=len(back)),
        out_shape=[
            jax.ShapeDtypeStruct((2 * rows, width), BF16),
            jax.ShapeDtypeStruct((rows, width), F32),
            jax.ShapeDtypeStruct((rows, width), F32),
            jax.ShapeDtypeStruct(later.shape, later.dtype),
        ],
        in_specs=[pl.BlockSpec(memory_space=pltpu.SMEM)]
        + [VMEM] * (1 + len(back))
        + [ANY] * (len(behind) + 1),
        out_specs=[VMEM] * 3 + [ANY],
        input_output_aliases={2 + len(back) + len(behind): 3},
        scratch_shapes=[pltpu.VMEM(kv.shape, F32)],
        compiler_params=pltpu.CompilerParams(vmem_limit_bytes=16 * 2**20),
        cost_estimate=SMALL,
        name="join",
    )(ranks, kv, *back, *behind, later)


def inner_kernel(rest_ref, got_ref, next_ref, *refs, pieces):
    query_refs, out_ref = refs[:pieces], refs[-2]
    rows, cols = query_refs[0].shape
    for i, ref in enumerate(query_refs):
        out_ref[:, i * cols : (i + 1) * cols] = ref[...]
    kv = rest_ref[...] + got_ref[:rows, :].astype(F32) + next_ref[...].astype(F32)
    out_ref[:, pieces * cols :] = kv.astype(BF16)


def inner_grads(rest, got, from_next, queries, later, behind):
    rows, cols = queries[0].shape
    return pl.pallas_call(
        functools.partial(inner_kernel, pieces=len(queries)),
        out_shape=[
            jax.ShapeDtypeStruct((rows, cols * len(queries) + rest.shape[1]), BF16),
            jax.ShapeDtypeStruct(later.shape, later.dtype),
        ],
        in_specs=[VMEM] * (3 + len(queries)) + [ANY] * (1 + len(behind)),
        out_specs=[VMEM, ANY],
        input_output_aliases={3 + len(queries): 1},
        compiler_params=pltpu.CompilerParams(vmem_limit_bytes=16 * 2**20),
        cost_estimate=SMALL,
        name="inner",
    )(rest, got, from_next, *queries, later, *behind)


def outer_kernel(*refs, tokens, atts, weights):
    held, att_held = refs[-2:]
    *own_refs, pair_ref, whole_ref = refs[-4 - len(TENSOR_ORDER) : -2]
    width, cols = own_refs[0].shape
    weight_refs = refs[tokens + atts : tokens + atts + weights]
    for block_refs, whole in (
        (refs[:tokens], held), (refs[tokens : tokens + atts], att_held), (weight_refs, whole_ref),
    ):
        start, columns = 0, whole.shape[1]
        for ref in block_refs:
            whole[start : start + ref.shape[0], :] = ref[:, :columns]
            start += ref.shape[0]
    step = min(width, 256)
    for e in range(0, width, step):
        at = slice(e, e + step)
        total = contract(held[:, at], att_held[...], ((0,), (0,)))
        for j, ref in enumerate(own_refs):
            ref[at, :] = total[:, j * cols : (j + 1) * cols]
        pair_at = slice(width + e, width + e + step)
        pair_ref[at, :] = contract(held[:, pair_at], att_held[...], ((0,), (0,))).astype(BF16)


def outer(tokens, atts, weights, behind):
    width, columns = weights[0].shape[1], atts[0].shape[1]
    depth, cols = tokens[0].shape[0] * len(tokens), columns // len(TENSOR_ORDER)
    return pl.pallas_call(
        functools.partial(
            outer_kernel, tokens=len(tokens), atts=len(atts), weights=len(weights)
        ),
        out_shape=[jax.ShapeDtypeStruct((width, cols), F32)] * len(TENSOR_ORDER)
        + [
            jax.ShapeDtypeStruct((width, columns), BF16),
            jax.ShapeDtypeStruct((sum(w.shape[0] for w in weights), width), BF16),
        ],
        in_specs=[VMEM] * (len(tokens) + len(atts) + len(weights)) + [ANY] * len(behind),
        out_specs=[VMEM] * (len(TENSOR_ORDER) + 2),
        scratch_shapes=[pltpu.VMEM((depth, 2 * width), BF16), pltpu.VMEM((depth, columns), BF16)],
        compiler_params=pltpu.CompilerParams(vmem_limit_bytes=40 * 2**20),
        cost_estimate=SMALL,
        name="outer",
    )(*tokens, *atts, *weights, *behind)


def add_pair_kernel(*refs, addends):
    own_ref, pair_ref, out_ref = refs[0], refs[1], refs[-1]
    total = own_ref[...] + pair_ref[...].astype(F32)
    for ref in refs[2:addends]:
        total = total + ref[...].astype(F32)
    out_ref[...] = total.astype(out_ref.dtype)


def add_pair(own, pair, block, others, dtype, behind):
    columns = pl.BlockSpec(own.shape, lambda i: (0, block))
    whole = pl.BlockSpec(own.shape, lambda i: (0, 0))
    return pl.pallas_call(
        functools.partial(add_pair_kernel, addends=2 + len(others)),
        grid=(1,),
        out_shape=jax.ShapeDtypeStruct(own.shape, dtype),
        in_specs=[whole, columns] + [whole] * len(others) + [ANY] * len(behind),
        out_specs=whole,
        compiler_params=pltpu.CompilerParams(vmem_limit_bytes=16 * 2**20),
        cost_estimate=SMALL,
        name="add_pair",
    )(own, pair, *others, *behind)


def feed_kernel(ranks_ref, *refs, tokens, pieces, distance):
    inner_refs, refs = refs[:tokens], refs[tokens:]
    weights, refs = [refs[i * pieces : (i + 1) * pieces] for i in range(2)], refs[2 * pieces :]
    out_refs, (held, last, sems) = refs[-3 - tokens : -3], refs[-3:]
    rows, columns = inner_refs[0].shape
    width = last.shape[1] // 2
    depth = refs[0].shape[0]
    copies = []
    for half in range(2):
        owner = lax.bitwise_xor(ranks_ref[0], half * distance)
        at = pl.ds(pl.multiple_of(owner * width, width), width)
        for i, ref in enumerate(refs[:2]):
            copies.append(
                pltpu.make_async_copy(
                    ref.at[:, at],
                    last.at[i * depth : (i + 1) * depth, half * width : (half + 1) * width],
                    sems.at[2 * half + i],
                )
            )
    for copy in copies:
        copy.start()
    for i, ref in enumerate(inner_refs):
        held[i * rows : (i + 1) * rows, :] = ref[...]
    for copy in copies:
        copy.wait()
    step = min(width, 512)
    for half in range(2):
        for start in range(0, width, step):
            at = slice(half * width + start, half * width + start + step)
            total = contract(held[:, columns - 2 * depth :], last[:, at], ((1,), (0,)))
            done = 0
            for w in weights[half]:
                part = held[:, done : done + w.shape[0]]
                total = total + contract(part, w[:, start : start + step], ((1,), (0,)))
                done += w.shape[0]
            for i, ref in enumerate(out_refs):
                ref[:, at] = total[i * rows : (i + 1) * rows].astype(BF16)


def feed(ranks, inners, own, pair, w_key, w_value, distance, behind):
    rows, columns = inners[0].shape
    width = own[0].shape[1]
    return pl.pallas_call(
        functools.partial(feed_kernel, tokens=len(inners), pieces=len(own), distance=distance),
        out_shape=[jax.ShapeDtypeStruct((rows, 2 * width), BF16)] * len(inners),
        in_specs=[pl.BlockSpec(memory_space=pltpu.SMEM)]
        + [VMEM] * (len(inners) + 2 * len(own))
        + [ANY] * (2 + len(behind)),
        out_specs=[VMEM] * len(inners),
        scratch_shapes=[
            pltpu.VMEM((rows * len(inners), columns), BF16),
            pltpu.VMEM((2 * w_key.shape[0], 2 * width), BF16),
            pltpu.SemaphoreType.DMA((4,)),
        ],
        compiler_params=pltpu.CompilerParams(vmem_limit_bytes=60 * 2**20),
        cost_estimate=SMALL,
        name="feed",
    )(ranks, *inners, *own, *pair, w_key, w_value, *behind)


def attention_kernel(
    ranks_ref, seg_query_ref, seg_key_ref, query_ref, attended_ref, key_ref, value_ref, log_ref,
    *refs, peers, befores, cycle_size,
):
    dout_refs, before_refs = refs[:peers], refs[peers : peers + befores]
    dquery_refs, away_refs = refs[-4 - befores - peers : -4 - befores], refs[-4 - befores : -4]
    kv_grads_ref, att_own_ref, dout_held, dquery_held = refs[-4:]
    rank, last_rank = ranks_ref[1], ranks_ref[2] == cycle_size - 1
    head_dim = key_ref.shape[1]
    span = query_ref.shape[0] // 2
    heads = query_ref.shape[1] // head_dim
    sub = 2 * span // peers
    inv_root = 1.0 / math.sqrt(head_dim)

    def place(a):
        return pl.ds(pl.multiple_of(a * sub, sub), sub)

    def by_head(x):
        return jnp.concatenate(
            [x[:, h * head_dim : (h + 1) * head_dim] for h in range(heads)], axis=0
        )

    cols = query_ref.shape[1]
    for i, (j, ref) in enumerate(zip(TENSOR_ORDER, dout_refs)):
        dout_held[place(lax.bitwise_xor(rank, j)), :] = ref[:sub, :]
        att_own_ref[:, i * cols : (i + 1) * cols] = ref[sub:, :] if j else attended_ref[place(rank), :]
    before = []
    for b in range(2):
        rows = slice(b * span, (b + 1) * span)
        query = by_head(query_ref[rows, :])
        dout = by_head(dout_held[rows, :])
        attended = by_head(attended_ref[rows, :])
        key_before = before_refs[b % befores][:, :head_dim]
        value_before = before_refs[b % befores][:, head_dim:]
        if b == 1:
            key_before = jnp.where(last_rank, key_ref[:span, :], key_before)
            value_before = jnp.where(last_rank, value_ref[:span, :], value_before)
        key = jnp.concatenate([key_before, key_ref[rows, :]], axis=0)
        value = jnp.concatenate([value_before, value_ref[rows, :]], axis=0)
        log_rows = jnp.concatenate([log_ref[rows, h : h + 1] for h in range(heads)], axis=0)
        query_at = lax.broadcasted_iota(jnp.int32, (span, 2 * span), 0)
        key_at = lax.broadcasted_iota(jnp.int32, (span, 2 * span), 1) - span
        allowed = (key_at <= query_at) & (seg_query_ref[rows, :] == seg_key_ref[b : b + 1, :])
        allowed = jnp.concatenate([allowed] * heads, axis=0)
        scores = contract(query, key, ((1,), (1,))) * inv_root
        prob = jnp.where(allowed, jnp.exp(scores - log_rows), 0.0)
        delta = jnp.sum(dout.astype(F32) * attended.astype(F32), axis=1, keepdims=True)
        dprob = contract(dout, value, ((1,), (1,)))
        dscore = (prob * (dprob - delta)).astype(BF16)
        dquery = (contract(dscore, key, ((1,), (0,))) * inv_root).astype(BF16)
        for h in range(heads):
            dquery_held[rows, h * head_dim : (h + 1) * head_dim] = dquery[
                h * span : (h + 1) * span
            ]
        key_grads = contract(dscore, query, ((0,), (0,))) * inv_root
        value_grads = contract(prob.astype(BF16), dout, ((0,), (0,)))
        kv_grads_ref[rows, :head_dim] = key_grads[span:]
        kv_grads_ref[rows, head_dim:] = value_grads[span:]
        before.append((key_grads[:span], value_grads[:span]))
    for i, half in enumerate((slice(0, head_dim), slice(head_dim, 2 * head_dim))):
        low, high = before[0][i], before[1][i]
        kv_grads_ref[:span, half] = kv_grads_ref[:span, half] + jnp.where(last_rank, high, 0.0)
        if befores == 1:
            away_refs[0][:, half] = jnp.where(last_rank, low, high).astype(BF16)
        else:
            away_refs[0][:, half] = low.astype(BF16)
            away_refs[1][:, half] = jnp.where(last_rank, 0.0, high).astype(BF16)
    for j, ref in zip(TENSOR_ORDER, dquery_refs):
        ref[...] = dquery_held[place(lax.bitwise_xor(rank, j)), :]


def attention(
    ranks, seg_query, seg_key, queries, attended, keys, values, log_sums, dout, before, behind,
    cycle_size,
):
    kv_shape = (keys.shape[0], 2 * keys.shape[1])
    return pl.pallas_call(
        functools.partial(
            attention_kernel, peers=len(dout), befores=len(before), cycle_size=cycle_size
        ),
        out_shape=[jax.ShapeDtypeStruct(dout[0].shape, BF16) for _ in dout]
        + [jax.ShapeDtypeStruct(x.shape, BF16) for x in before]
        + [
            jax.ShapeDtypeStruct(kv_shape, F32),
            jax.ShapeDtypeStruct((dout[0].shape[0], len(dout) * dout[0].shape[1]), BF16),
        ],
        in_specs=[pl.BlockSpec(memory_space=pltpu.SMEM)]
        + [VMEM] * (7 + len(dout) + len(before))
        + [ANY] * len(behind),
        out_specs=[VMEM] * (len(dout) + len(before) + 2),
        scratch_shapes=[pltpu.VMEM(queries.shape, BF16)] * 2,
        compiler_params=pltpu.CompilerParams(vmem_limit_bytes=32 * 2**20),
        cost_estimate=SMALL,
        name="attention",
    )(ranks, seg_query, seg_key, queries, attended, keys, values, log_sums, *dout, *before, *behind)


def on_device(
    grad_out, queries, attended, keys, values, log_sums, segment_ids, w_out, w_query, w_key, w_value
):
    tensor_rank = lax.axis_index("tensor")
    plane_rank = lax.axis_index(PLANE)
    cycle_size, cycle_pos = lax.axis_size("context"), lax.axis_index("context")
    own_rows, features = grad_out.shape
    width = w_out.shape[0]
    cols = queries.shape[1]
    span = queries.shape[0] // 2
    pair = cycle_size
    bits = [1 << i for i in range(lax.axis_size(PLANE).bit_length() - 1)]
    bits = [bit for bit in reversed(bits) if bit != pair]
    meets = [0]
    for bit in bits:
        meets += [k ^ bit for k in meets]
    meets = meets[1:]

    def plane_gather(x, name):
        return [x] + [swapped(x, PLANE, k, f"{name}_{k}") for k in meets]

    def along(x, j, name):
        return swapped(x, "tensor", j, f"{name}_{j}")

    def across(x, name):
        return swapped(x, PLANE, pair, name)

    out_2, out_1 = along(w_out, 2, "w_out"), along(w_out, 1, "w_out")

    ranks = jnp.stack([plane_rank, tensor_rank, cycle_pos])
    carrier = meets.index(1) + 1 if cycle_size == 2 else None
    tokens = cut(ranks, grad_out, keys, values, [0] + meets, pair, width, carrier)
    tokens = [tokens[0]] + [swapped(x, PLANE, k, f"tokens_{k}") for k, x in zip(meets, tokens[1:])]
    out_2 = hand_on([out_2], [], FLOPS // 10)[0]
    out_2 = hand_on([out_2], tokens[1:2])[0]
    out_1 = hand_on([out_1], tokens[2:], FLOPS)[0]
    w_out_own = [w_out, out_2, out_1, along(out_2, 1, "w_out_on")]
    w_out_pair = [across(w, f"w_out_pair_{i}") for i, w in enumerate(w_out_own)]

    query_2, query_1 = along(w_query, 2, "w_query"), along(w_query, 1, "w_query")

    seg_row = segment_ids[0]
    high_span = 2 * cycle_size - 1 - cycle_pos

    def seg_slice(at):
        return lax.dynamic_slice_in_dim(seg_row, jnp.maximum(at, 0) * span, span)

    seg_low, seg_high = seg_slice(cycle_pos), seg_slice(high_span)
    seg_before = jnp.where(cycle_pos == 0, -1, seg_slice(cycle_pos - 1))
    seg_query = jnp.concatenate([seg_low, seg_high])[:, None]
    seg_key = jnp.stack(
        [
            jnp.concatenate([seg_before, seg_low]),
            jnp.concatenate([seg_slice(high_span - 1), seg_high]),
        ]
    )
    log_rows = log_sums.T

    partial_attn = project(tokens, w_out_own, w_out_pair, carrier)
    partial_attn, before = partial_attn[: len(tokens)], partial_attn[len(tokens) :]
    if cycle_size != 2:
        kv_pair = jnp.concatenate([keys, values], axis=1)
        before = neighbours(kv_pair[span:], kv_pair[:span])
    parts = [swapped(x, PLANE, k, f"attn_{k}") for k, x in zip(meets, partial_attn[1:])]
    dout = add_up(ranks, partial_attn[0], attended, parts)
    dout = [dout[0]] + [along(x, j, "dout") for x, j in zip(dout[1:], TENSOR_ORDER[1:])]
    *dquery, kv_grads, att_own = attention(
        ranks, seg_query, seg_key, queries, attended, keys, values, log_rows, dout, before,
        [query_2, query_1], cycle_size,
    )
    dquery, away = dquery[:4], dquery[4:]

    dquery = dquery[:1] + [along(x, j, "dquery") for x, j in zip(dquery[1:], TENSOR_ORDER[1:])]
    back = [swapped(away[0], "context", 1, "kv_back")] if cycle_size == 2 else neighbours(*away)
    kv_away, kv_next, kv_rest, att_own = join(ranks, kv_grads, back, dquery[1:], att_own)
    att_met = plane_gather(att_own, "attended")
    att_met[1:] = hand_on(att_met[1:], [], FLOPS // 10)
    got = along(kv_away, 2, "kv")
    kv_next = along((kv_next + got[own_rows:].astype(F32)).astype(BF16), 1, "kv")
    inner, query_2 = inner_grads(
        kv_rest, got, kv_next, dquery, query_2, []
    )
    inner_met = plane_gather(inner, "inner")

    *out_own, out_pair, w_query_own = outer(
        tokens, att_met, [w_query, query_2, query_1], [inner]
    )
    query_3 = along(query_2, 1, "w_query_on")

    out_pair = across(out_pair, "out_proj_pair")
    to_3 = add_pair(out_own[3], out_pair, 3, [], BF16, [])
    from_3 = along(to_3, 1, "out_proj_3")
    *inner_met[1:], query_3 = hand_on([*inner_met[1:], query_3], [], FLOPS)
    *inner_met[1:], query_3 = hand_on([*inner_met[1:], query_3], [out_pair])
    w_query_own = [w_query_own, query_3]
    w_query_pair = [across(w, f"w_query_pair_{i}") for i, w in enumerate(w_query_own)]

    blocks = feed(
        ranks, inner_met, w_query_own, w_query_pair, w_key, w_value, pair, [to_3]
    )
    to_1 = add_pair(out_own[2], out_pair, 2, [], BF16, [to_3])
    to_2 = add_pair(out_own[1], out_pair, 1, [from_3], BF16, [blocks[1]])
    out_proj_grad = add_pair(
        out_own[0], out_pair, 0, [along(to_1, 1, "out_proj"), along(to_2, 2, "out_proj")], F32, []
    )
    blocks = [(0, blocks[0])] + [(k, swapped(x, PLANE, k, f"grads_{k}")) for k, x in zip(meets, blocks[1:])]
    received = hand_on([x for _, x in blocks[1:]], [], FLOPS)
    blocks = blocks[:1] + list(zip(meets, received))
    grad_input = jnp.zeros((own_rows, features), BF16)
    for k, block in blocks:
        for i, owner in enumerate((plane_rank ^ k, plane_rank ^ k ^ pair)):
            grad_input = lax.dynamic_update_slice_in_dim(
                grad_input, block[:, i * width : (i + 1) * width], owner * width, axis=1
            )
    return (grad_input, out_proj_grad)


def solution(mesh):
    placed = (
        P(("dp", "context", "tensor"), None),
        P(("dp", "context"), "tensor"),
        P(("dp", "context"), "tensor"),
        P(("dp", "context"), None),
        P(("dp", "context"), None),
        P("tensor", ("dp", "context")),
        P("dp", None),
        P(("dp", "context"), "tensor"),
        P("tensor", ("dp", "context")),
        P(),
        P(),
    )
    return jax.shard_map(
        on_device,
        mesh=mesh,
        in_specs=placed,
        out_specs=(P(("dp", "context", "tensor"), None), P(("dp", "context"), "tensor")),
        check_vma=False,
    )
```

```python
import functools
import math

import jax
import jax.numpy as jnp
from jax import lax
from jax.experimental import pallas as pl
from jax.experimental.pallas import tpu as pltpu
from jax.sharding import PartitionSpec as P

PLANE = ("dp", "context")
BF16 = jnp.bfloat16
F32 = jnp.float32
TENSOR_ORDER = (0, 2, 1, 3)


def swapped(x, axes, bit, name):
    size = lax.axis_size(axes)
    with jax.named_scope(name):
        return lax.ppermute(x, axes, [(i, i ^ bit) for i in range(size)])


def neighbours(to_left, to_right):
    size = lax.axis_size("context")
    up = [(i, i + 1) for i in range(size - 1)]
    down = [(i + 1, i) for i in range(size - 1)]
    return [lax.ppermute(to_right, "context", up), lax.ppermute(to_left, "context", down)]


def contract(x, y, dims):
    return lax.dot_general(x, y, (dims, ((), ())), preferred_element_type=F32)


VMEM = pl.BlockSpec(memory_space=pltpu.VMEM)
ANY = pl.BlockSpec(memory_space=pl.ANY)
FLOPS = 4 * 10**10
SMALL = pl.CostEstimate(flops=0, bytes_accessed=0, transcendentals=0)


def cut_kernel(
    ranks_ref, x_ref, key_ref, value_ref, weight_ref, *refs, parts, pair, width, carrier
):
    out_refs, weight_out_ref, sems = refs[:-2], refs[-2], refs[-1]
    moves = [(weight_ref, weight_out_ref)]
    for i, k in enumerate(parts):
        for half in range(2):
            owner = lax.bitwise_xor(ranks_ref[0], k ^ (half * pair))
            start = pl.multiple_of(owner * width, width)
            moves.append(
                (x_ref.at[:, pl.ds(start, width)], out_refs[i].at[:, half * width : (half + 1) * width])
            )
    if carrier is not None:
        rows, start = x_ref.shape[0], 2 * width
        for half in range(2):
            at = pl.ds(pl.multiple_of((2 * ranks_ref[2] + half) * rows, rows), rows)
            for ref in (key_ref, value_ref):
                end = start + ref.shape[1]
                moves.append((ref.at[at, :], out_refs[carrier].at[:, start:end]))
                start = end
    copies = [pltpu.make_async_copy(x, y, sems.at[i]) for i, (x, y) in enumerate(moves)]
    for copy in copies:
        copy.start()
    for copy in copies:
        copy.wait()


def cut(ranks, x, keys, values, weight, parts, pair, carrier):
    rows, width = x.shape[0], weight.shape[0]
    extra = 2 * (keys.shape[1] + values.shape[1])
    return pl.pallas_call(
        functools.partial(cut_kernel, parts=parts, pair=pair, width=width, carrier=carrier),
        out_shape=[
            jax.ShapeDtypeStruct((rows, 2 * width + (extra if i == carrier else 0)), x.dtype)
            for i in range(len(parts))
        ]
        + [jax.ShapeDtypeStruct(weight.shape, weight.dtype)],
        in_specs=[pl.BlockSpec(memory_space=pltpu.SMEM)] + [ANY] * 4,
        out_specs=[VMEM] * (len(parts) + 1),
        scratch_shapes=[pltpu.SemaphoreType.DMA((2 * len(parts) + 5,))],
        compiler_params=pltpu.CompilerParams(vmem_limit_bytes=60 * 2**20),
        cost_estimate=SMALL,
        name="cut",
    )(ranks, x, keys, values, weight)


def project_kernel(*refs, tokens, pieces, carrier):
    token_refs, refs = refs[:tokens], refs[tokens:]
    own_refs, pair_refs, refs = refs[:pieces], refs[pieces : 2 * pieces], refs[2 * pieces :]
    out_refs, held = refs[:tokens], refs[-1]
    rows = token_refs[0].shape[0]
    width, cols = own_refs[0].shape
    for i, ref in enumerate(token_refs):
        held[i * rows : (i + 1) * rows, :] = ref[:, : 2 * width]
    if carrier is not None:
        before_ref = refs[tokens]
        depth = before_ref.shape[1]
        for half in range(2):
            start = 2 * width + half * depth
            before_ref[half * rows : (half + 1) * rows, :] = token_refs[carrier][
                :, start : start + depth
            ]
    for j in range(pieces):
        total = contract(held[:, :width], own_refs[j][...], ((1,), (0,)))
        total = total + contract(held[:, width:], pair_refs[j][...], ((1,), (0,)))
        for i, ref in enumerate(out_refs):
            ref[:, j * cols : (j + 1) * cols] = total[i * rows : (i + 1) * rows].astype(ref.dtype)


def project(tokens, own, pair, carrier):
    rows = tokens[0].shape[0]
    width, cols = own[0].shape
    out_shape = [
        jax.ShapeDtypeStruct((rows, len(own) * cols), BF16 if i else F32)
        for i in range(len(tokens))
    ]
    if carrier is not None:
        extra = (tokens[carrier].shape[1] - 2 * width) // 2
        out_shape.append(jax.ShapeDtypeStruct((2 * rows, extra), BF16))
    return pl.pallas_call(
        functools.partial(
            project_kernel, tokens=len(tokens), pieces=len(own), carrier=carrier
        ),
        out_shape=out_shape,
        in_specs=[VMEM] * (len(tokens) + 2 * len(own)),
        out_specs=[VMEM] * len(out_shape),
        scratch_shapes=[pltpu.VMEM((rows * len(tokens), 2 * width), BF16)],
        compiler_params=pltpu.CompilerParams(vmem_limit_bytes=20 * 2**20),
        cost_estimate=SMALL,
        name="project",
    )(*tokens, *own, *pair)


def hand_on_kernel(*refs):
    pass


def hand_on(arrays, behind, flops=0):
    return pl.pallas_call(
        hand_on_kernel,
        out_shape=[jax.ShapeDtypeStruct(x.shape, x.dtype) for x in arrays],
        in_specs=[ANY] * (len(arrays) + len(behind)),
        out_specs=[ANY] * len(arrays),
        input_output_aliases={i: i for i in range(len(arrays))},
        compiler_params=pltpu.CompilerParams(vmem_limit_bytes=16 * 2**20),
        cost_estimate=pl.CostEstimate(flops=flops, bytes_accessed=0, transcendentals=0),
        name="hand_on",
    )(*arrays, *behind)


def add_kernel(ranks_ref, own_ref, att_ref, *refs, parts):
    part_refs, out_refs, share_refs = refs[:parts], refs[parts : -4], refs[-4:]
    rows, cols = out_refs[0].shape
    total = own_ref[...]
    for ref in part_refs:
        total = total + ref[...].astype(F32)
    for j, ref in enumerate(out_refs):
        ref[...] = total[:, j * cols : (j + 1) * cols].astype(BF16)
    for j, ref in zip(TENSOR_ORDER, share_refs):
        owner = lax.bitwise_xor(ranks_ref[1], j)
        ref[...] = att_ref[pl.ds(pl.multiple_of(owner * rows, rows), rows), :]


def add_up(ranks, own, attended, parts):
    rows, cols = own.shape[0], attended.shape[1]
    peers = len(TENSOR_ORDER)
    return pl.pallas_call(
        functools.partial(add_kernel, parts=len(parts)),
        out_shape=[jax.ShapeDtypeStruct((rows, cols), BF16)] * (2 * peers),
        in_specs=[pl.BlockSpec(memory_space=pltpu.SMEM)] + [VMEM] * (2 + len(parts)),
        out_specs=[VMEM] * (2 * peers),
        compiler_params=pltpu.CompilerParams(vmem_limit_bytes=60 * 2**20),
        cost_estimate=SMALL,
        name="add_up",
    )(ranks, own, attended, *parts)


def join_kernel(ranks_ref, kv_ref, *refs, backs, atts):
    back_refs, att_refs = refs[:backs], refs[backs : backs + atts]
    (away_ref, next_ref, own_ref, att_own_ref), held = refs[-5:-1], refs[-1]
    cols = att_refs[0].shape[1]
    for i, ref in enumerate(att_refs):
        att_own_ref[:, i * cols : (i + 1) * cols] = ref[...]
    rows = own_ref.shape[0]
    span = kv_ref.shape[0] // 2
    held[...] = kv_ref[...]
    if backs == 1:
        at = pl.ds(pl.multiple_of(ranks_ref[2] * span, span), span)
        held[at, :] = held[at, :] + back_refs[0][...].astype(F32)
    else:
        held[span:, :] = held[span:, :] + back_refs[0][...].astype(F32)
        held[:span, :] = held[:span, :] + back_refs[1][...].astype(F32)

    def rank_rows(j):
        at = pl.ds(pl.multiple_of(lax.bitwise_xor(ranks_ref[1], j) * rows, rows), rows)
        return held[at, :]

    away_ref[:rows, :] = rank_rows(2).astype(BF16)
    away_ref[rows:, :] = rank_rows(3).astype(BF16)
    next_ref[...] = rank_rows(1)
    own_ref[...] = rank_rows(0)


def join(ranks, kv, back, atts, behind):
    rows, width = kv.shape[0] // len(TENSOR_ORDER), kv.shape[1]
    return pl.pallas_call(
        functools.partial(join_kernel, backs=len(back), atts=len(atts)),
        out_shape=[
            jax.ShapeDtypeStruct((2 * rows, width), BF16),
            jax.ShapeDtypeStruct((rows, width), F32),
            jax.ShapeDtypeStruct((rows, width), F32),
            jax.ShapeDtypeStruct((rows, len(atts) * atts[0].shape[1]), BF16),
        ],
        in_specs=[pl.BlockSpec(memory_space=pltpu.SMEM)]
        + [VMEM] * (1 + len(back) + len(atts))
        + [ANY] * len(behind),
        out_specs=[VMEM] * 4,
        scratch_shapes=[pltpu.VMEM(kv.shape, F32)],
        compiler_params=pltpu.CompilerParams(vmem_limit_bytes=8 * 2**20),
        cost_estimate=SMALL,
        name="join",
    )(ranks, kv, *back, *atts, *behind)


def inner_kernel(rest_ref, got_ref, next_ref, *refs, pieces):
    query_refs, out_ref = refs[:pieces], refs[-2]
    rows, cols = query_refs[0].shape
    for i, ref in enumerate(query_refs):
        out_ref[:, i * cols : (i + 1) * cols] = ref[...]
    kv = rest_ref[...] + got_ref[:rows, :].astype(F32) + next_ref[...].astype(F32)
    out_ref[:, pieces * cols :] = kv.astype(BF16)


def inner_grads(rest, got, from_next, queries, later, behind):
    rows, cols = queries[0].shape
    return pl.pallas_call(
        functools.partial(inner_kernel, pieces=len(queries)),
        out_shape=[
            jax.ShapeDtypeStruct((rows, cols * len(queries) + rest.shape[1]), BF16),
            jax.ShapeDtypeStruct(later.shape, later.dtype),
        ],
        in_specs=[VMEM] * (3 + len(queries)) + [ANY] * (1 + len(behind)),
        out_specs=[VMEM, ANY],
        input_output_aliases={3 + len(queries): 1},
        compiler_params=pltpu.CompilerParams(vmem_limit_bytes=8 * 2**20),
        cost_estimate=SMALL,
        name="inner",
    )(rest, got, from_next, *queries, later, *behind)


def outer_kernel(*refs, tokens, atts, weights):
    held, att_held = refs[-2:]
    *own_refs, pair_ref, whole_ref = refs[-4 - len(TENSOR_ORDER) : -2]
    width, cols = own_refs[0].shape
    weight_refs = refs[tokens + atts : tokens + atts + weights]
    for block_refs, whole in (
        (refs[:tokens], held), (refs[tokens : tokens + atts], att_held), (weight_refs, whole_ref),
    ):
        start, columns = 0, whole.shape[1]
        for ref in block_refs:
            whole[start : start + ref.shape[0], :] = ref[:, :columns]
            start += ref.shape[0]
    step = min(width, 256)
    for e in range(0, width, step):
        at = slice(e, e + step)
        total = contract(held[:, at], att_held[...], ((0,), (0,)))
        for j, ref in enumerate(own_refs):
            ref[at, :] = total[:, j * cols : (j + 1) * cols]
        pair_at = slice(width + e, width + e + step)
        pair_ref[at, :] = contract(held[:, pair_at], att_held[...], ((0,), (0,))).astype(BF16)


def outer(tokens, atts, weights, behind):
    width, columns = weights[0].shape[1], atts[0].shape[1]
    depth, cols = tokens[0].shape[0] * len(tokens), columns // len(TENSOR_ORDER)
    return pl.pallas_call(
        functools.partial(
            outer_kernel, tokens=len(tokens), atts=len(atts), weights=len(weights)
        ),
        out_shape=[jax.ShapeDtypeStruct((width, cols), F32)] * len(TENSOR_ORDER)
        + [
            jax.ShapeDtypeStruct((width, columns), BF16),
            jax.ShapeDtypeStruct((sum(w.shape[0] for w in weights), width), BF16),
        ],
        in_specs=[VMEM] * (len(tokens) + len(atts) + len(weights)) + [ANY] * len(behind),
        out_specs=[VMEM] * (len(TENSOR_ORDER) + 2),
        scratch_shapes=[pltpu.VMEM((depth, 2 * width), BF16), pltpu.VMEM((depth, columns), BF16)],
        compiler_params=pltpu.CompilerParams(vmem_limit_bytes=20 * 2**20),
        cost_estimate=SMALL,
        name="outer",
    )(*tokens, *atts, *weights, *behind)


def add_pair_kernel(*refs, addends):
    own_ref, pair_ref, out_ref = refs[0], refs[1], refs[-1]
    total = own_ref[...] + pair_ref[...].astype(F32)
    for ref in refs[2:addends]:
        total = total + ref[...].astype(F32)
    out_ref[...] = total.astype(out_ref.dtype)


def add_pair(own, pair, block, others, dtype, behind):
    columns = pl.BlockSpec(own.shape, lambda i: (0, block))
    whole = pl.BlockSpec(own.shape, lambda i: (0, 0))
    return pl.pallas_call(
        functools.partial(add_pair_kernel, addends=2 + len(others)),
        grid=(1,),
        out_shape=jax.ShapeDtypeStruct(own.shape, dtype),
        in_specs=[whole, columns] + [whole] * len(others) + [ANY] * len(behind),
        out_specs=whole,
        compiler_params=pltpu.CompilerParams(vmem_limit_bytes=16 * 2**20),
        cost_estimate=SMALL,
        name="add_pair",
    )(own, pair, *others, *behind)


def feed_kernel(ranks_ref, *refs, tokens, pieces, distance):
    inner_refs, refs = refs[:tokens], refs[tokens:]
    weights, refs = [refs[i * pieces : (i + 1) * pieces] for i in range(2)], refs[2 * pieces :]
    out_refs, (held, last, sems) = refs[-3 - tokens : -3], refs[-3:]
    rows, columns = inner_refs[0].shape
    width = last.shape[1] // 2
    depth = refs[0].shape[0]
    copies = []
    for half in range(2):
        owner = lax.bitwise_xor(ranks_ref[0], half * distance)
        at = pl.ds(pl.multiple_of(owner * width, width), width)
        for i, ref in enumerate(refs[:2]):
            copies.append(
                pltpu.make_async_copy(
                    ref.at[:, at],
                    last.at[i * depth : (i + 1) * depth, half * width : (half + 1) * width],
                    sems.at[2 * half + i],
                )
            )
    for copy in copies:
        copy.start()
    for i, ref in enumerate(inner_refs):
        held[i * rows : (i + 1) * rows, :] = ref[...]
    for copy in copies:
        copy.wait()
    step = min(width, 512)
    for half in range(2):
        for start in range(0, width, step):
            at = slice(half * width + start, half * width + start + step)
            total = contract(held[:, columns - 2 * depth :], last[:, at], ((1,), (0,)))
            done = 0
            for w in weights[half]:
                part = held[:, done : done + w.shape[0]]
                total = total + contract(part, w[:, start : start + step], ((1,), (0,)))
                done += w.shape[0]
            for i, ref in enumerate(out_refs):
                ref[:, at] = total[i * rows : (i + 1) * rows].astype(BF16)


def feed(ranks, inners, own, pair, w_key, w_value, distance, behind):
    rows, columns = inners[0].shape
    width = own[0].shape[1]
    return pl.pallas_call(
        functools.partial(feed_kernel, tokens=len(inners), pieces=len(own), distance=distance),
        out_shape=[jax.ShapeDtypeStruct((rows, 2 * width), BF16)] * len(inners),
        in_specs=[pl.BlockSpec(memory_space=pltpu.SMEM)]
        + [VMEM] * (len(inners) + 2 * len(own))
        + [ANY] * (2 + len(behind)),
        out_specs=[VMEM] * len(inners),
        scratch_shapes=[
            pltpu.VMEM((rows * len(inners), columns), BF16),
            pltpu.VMEM((2 * w_key.shape[0], 2 * width), BF16),
            pltpu.SemaphoreType.DMA((4,)),
        ],
        compiler_params=pltpu.CompilerParams(vmem_limit_bytes=20 * 2**20),
        cost_estimate=SMALL,
        name="feed",
    )(ranks, *inners, *own, *pair, w_key, w_value, *behind)


def place_kernel(ranks_ref, *refs, parts, distance):
    out_ref, sems = refs[-2], refs[-1]
    width = refs[0].shape[1] // 2
    copies = []
    for i, (k, ref) in enumerate(zip(parts, refs)):
        for half in range(2):
            owner = lax.bitwise_xor(ranks_ref[0], k ^ (half * distance))
            at = pl.ds(pl.multiple_of(owner * width, width), width)
            copies.append(
                pltpu.make_async_copy(
                    ref.at[:, half * width : (half + 1) * width],
                    out_ref.at[:, at],
                    sems.at[2 * i + half],
                )
            )
    for copy in copies:
        copy.start()
    for copy in copies:
        copy.wait()


def place_blocks(ranks, blocks, parts, distance, features, out):
    given = [] if out is None else [out]
    return pl.pallas_call(
        functools.partial(place_kernel, parts=parts, distance=distance),
        out_shape=jax.ShapeDtypeStruct((blocks[0].shape[0], features), BF16),
        in_specs=[pl.BlockSpec(memory_space=pltpu.SMEM)]
        + [VMEM] * len(blocks)
        + [ANY] * len(given),
        out_specs=ANY,
        scratch_shapes=[pltpu.SemaphoreType.DMA((2 * len(blocks),))],
        input_output_aliases={1 + len(blocks): 0} if given else {},
        compiler_params=pltpu.CompilerParams(vmem_limit_bytes=16 * 2**20),
        cost_estimate=SMALL,
        name="place",
    )(ranks, *blocks, *given)


def attention_kernel(
    ranks_ref, seg_query_ref, seg_key_ref, query_ref, attended_ref, key_ref, value_ref, log_ref,
    *refs, peers, befores, cycle_size,
):
    dout_refs, before_refs = refs[:peers], refs[peers : peers + befores]
    dquery_refs, away_refs = refs[-3 - befores - peers : -3 - befores], refs[-3 - befores : -3]
    kv_grads_ref, dout_held, dquery_held = refs[-3:]
    rank, last_rank = ranks_ref[1], ranks_ref[2] == cycle_size - 1
    head_dim = key_ref.shape[1]
    span = query_ref.shape[0] // 2
    heads = query_ref.shape[1] // head_dim
    sub = 2 * span // peers
    inv_root = 1.0 / math.sqrt(head_dim)

    def place(a):
        return pl.ds(pl.multiple_of(a * sub, sub), sub)

    def by_head(x):
        return jnp.concatenate(
            [x[:, h * head_dim : (h + 1) * head_dim] for h in range(heads)], axis=0
        )

    for j, ref in zip(TENSOR_ORDER, dout_refs):
        dout_held[place(lax.bitwise_xor(rank, j)), :] = ref[...]
    before = []
    for b in range(2):
        rows = slice(b * span, (b + 1) * span)
        query = by_head(query_ref[rows, :])
        dout = by_head(dout_held[rows, :])
        attended = by_head(attended_ref[rows, :])
        key_before = before_refs[b % befores][:, :head_dim]
        value_before = before_refs[b % befores][:, head_dim:]
        if b == 1:
            key_before = jnp.where(last_rank, key_ref[:span, :], key_before)
            value_before = jnp.where(last_rank, value_ref[:span, :], value_before)
        key = jnp.concatenate([key_before, key_ref[rows, :]], axis=0)
        value = jnp.concatenate([value_before, value_ref[rows, :]], axis=0)
        log_rows = jnp.concatenate([log_ref[rows, h : h + 1] for h in range(heads)], axis=0)
        query_at = lax.broadcasted_iota(jnp.int32, (span, 2 * span), 0)
        key_at = lax.broadcasted_iota(jnp.int32, (span, 2 * span), 1) - span
        allowed = (key_at <= query_at) & (seg_query_ref[rows, :] == seg_key_ref[b : b + 1, :])
        allowed = jnp.concatenate([allowed] * heads, axis=0)
        scores = contract(query, key, ((1,), (1,))) * inv_root
        prob = jnp.where(allowed, jnp.exp(scores - log_rows), 0.0)
        delta = jnp.sum(dout.astype(F32) * attended.astype(F32), axis=1, keepdims=True)
        dprob = contract(dout, value, ((1,), (1,)))
        dscore = (prob * (dprob - delta)).astype(BF16)
        dquery = (contract(dscore, key, ((1,), (0,))) * inv_root).astype(BF16)
        for h in range(heads):
            dquery_held[rows, h * head_dim : (h + 1) * head_dim] = dquery[
                h * span : (h + 1) * span
            ]
        key_grads = contract(dscore, query, ((0,), (0,))) * inv_root
        value_grads = contract(prob.astype(BF16), dout, ((0,), (0,)))
        kv_grads_ref[rows, :head_dim] = key_grads[span:]
        kv_grads_ref[rows, head_dim:] = value_grads[span:]
        before.append((key_grads[:span], value_grads[:span]))
    for i, half in enumerate((slice(0, head_dim), slice(head_dim, 2 * head_dim))):
        low, high = before[0][i], before[1][i]
        kv_grads_ref[:span, half] = kv_grads_ref[:span, half] + jnp.where(last_rank, high, 0.0)
        if befores == 1:
            away_refs[0][:, half] = jnp.where(last_rank, low, high).astype(BF16)
        else:
            away_refs[0][:, half] = low.astype(BF16)
            away_refs[1][:, half] = jnp.where(last_rank, 0.0, high).astype(BF16)
    for j, ref in zip(TENSOR_ORDER, dquery_refs):
        ref[...] = dquery_held[place(lax.bitwise_xor(rank, j)), :]


def attention(
    ranks, seg_query, seg_key, queries, attended, keys, values, log_sums, dout, before, behind,
    cycle_size,
):
    kv_shape = (keys.shape[0], 2 * keys.shape[1])
    return pl.pallas_call(
        functools.partial(
            attention_kernel, peers=len(dout), befores=len(before), cycle_size=cycle_size
        ),
        out_shape=[jax.ShapeDtypeStruct(dout[0].shape, BF16) for _ in dout]
        + [jax.ShapeDtypeStruct(x.shape, BF16) for x in before]
        + [jax.ShapeDtypeStruct(kv_shape, F32)],
        in_specs=[pl.BlockSpec(memory_space=pltpu.SMEM)]
        + [VMEM] * (7 + len(dout) + len(before))
        + [ANY] * len(behind),
        out_specs=[VMEM] * (len(dout) + len(before) + 1),
        scratch_shapes=[pltpu.VMEM(queries.shape, BF16)] * 2,
        compiler_params=pltpu.CompilerParams(vmem_limit_bytes=32 * 2**20),
        cost_estimate=SMALL,
        name="attention",
    )(ranks, seg_query, seg_key, queries, attended, keys, values, log_sums, *dout, *before, *behind)


def on_device(
    grad_out, queries, attended, keys, values, log_sums, segment_ids, w_out, w_query, w_key, w_value
):
    tensor_rank = lax.axis_index("tensor")
    plane_rank = lax.axis_index(PLANE)
    cycle_size, cycle_pos = lax.axis_size("context"), lax.axis_index("context")
    own_rows, features = grad_out.shape
    width = w_out.shape[0]
    cols = queries.shape[1]
    span = queries.shape[0] // 2
    pair = cycle_size
    bits = [1 << i for i in range(lax.axis_size(PLANE).bit_length() - 1)]
    bits = [bit for bit in reversed(bits) if bit != pair]
    meets = [0]
    for bit in bits:
        meets += [k ^ bit for k in meets]
    meets = meets[1:]

    def plane_gather(x, name):
        return [x] + [swapped(x, PLANE, k, f"{name}_{k}") for k in meets]

    def along(x, j, name):
        return swapped(x, "tensor", j, f"{name}_{j}")

    def across(x, name):
        return swapped(x, PLANE, pair, name)

    out_2, out_1 = along(w_out, 2, "w_out"), along(w_out, 1, "w_out")

    ranks = jnp.stack([plane_rank, tensor_rank, cycle_pos])
    carrier = meets.index(1) + 1 if cycle_size == 2 else None
    *tokens, w_out_copy = cut(ranks, grad_out, keys, values, w_out, [0] + meets, pair, carrier)
    tokens = [tokens[0]] + [swapped(x, PLANE, k, f"tokens_{k}") for k, x in zip(meets, tokens[1:])]
    out_2, out_1 = hand_on([out_2, out_1], [], FLOPS // 10)
    out_2, w_out_copy = hand_on([out_2, w_out_copy], tokens[1:2])
    out_1 = hand_on([out_1], tokens[2:], FLOPS)[0]
    w_out_own = [w_out_copy, out_2, out_1, along(out_2, 1, "w_out_on")]
    w_out_pair = [across(w, f"w_out_pair_{i}") for i, w in enumerate(w_out_own)]

    query_2, query_1 = along(w_query, 2, "w_query"), along(w_query, 1, "w_query")
    query_2, query_1 = hand_on([query_2, query_1], [], FLOPS // 10)

    seg_row = segment_ids[0]
    high_span = 2 * cycle_size - 1 - cycle_pos

    def seg_slice(at):
        return lax.dynamic_slice_in_dim(seg_row, jnp.maximum(at, 0) * span, span)

    seg_low, seg_high = seg_slice(cycle_pos), seg_slice(high_span)
    seg_before = jnp.where(cycle_pos == 0, -1, seg_slice(cycle_pos - 1))
    seg_query = jnp.concatenate([seg_low, seg_high])[:, None]
    seg_key = jnp.stack(
        [
            jnp.concatenate([seg_before, seg_low]),
            jnp.concatenate([seg_slice(high_span - 1), seg_high]),
        ]
    )
    log_rows = log_sums.T

    partial_attn = project(tokens, w_out_own, w_out_pair, carrier)
    partial_attn, before = partial_attn[: len(tokens)], partial_attn[len(tokens) :]
    if cycle_size != 2:
        kv_pair = jnp.concatenate([keys, values], axis=1)
        before = neighbours(kv_pair[span:], kv_pair[:span])
    parts = [swapped(x, PLANE, k, f"attn_{k}") for k, x in zip(meets, partial_attn[1:])]
    shared = add_up(ranks, partial_attn[0], attended, parts)
    dout, atts = shared[:4], shared[4:]
    dout = [dout[0]] + [along(x, j, "dout") for x, j in zip(dout[1:], TENSOR_ORDER[1:])]
    dout[1:] = hand_on(dout[1:], [], FLOPS // 10)
    atts = [along(x, j, "attended") for x, j in zip(atts[1:], TENSOR_ORDER[1:])]
    atts = [shared[4], *hand_on(atts, [], FLOPS // 10)]
    *dquery, kv_grads = attention(
        ranks, seg_query, seg_key, queries, attended, keys, values, log_rows, dout, before,
        [query_2, query_1], cycle_size,
    )
    dquery, away = dquery[:4], dquery[4:]

    dquery = dquery[:1] + [along(x, j, "dquery") for x, j in zip(dquery[1:], TENSOR_ORDER[1:])]
    back = [swapped(away[0], "context", 1, "kv_back")] if cycle_size == 2 else neighbours(*away)
    kv_away, kv_next, kv_rest, att_own = join(ranks, kv_grads, back, atts, dquery[1:])
    att_met = plane_gather(att_own, "attended")
    att_met[1:] = hand_on(att_met[1:], [], FLOPS // 10)
    got = along(kv_away, 2, "kv")
    kv_next = along((kv_next + got[own_rows:].astype(F32)).astype(BF16), 1, "kv")
    inner, query_2 = inner_grads(
        kv_rest, got, kv_next, dquery, query_2, []
    )
    inner_met = plane_gather(inner, "inner")

    *out_own, out_pair, w_query_own = outer(
        tokens, att_met, [w_query, query_2, query_1], [inner]
    )
    query_3 = along(query_2, 1, "w_query_on")

    out_pair = across(out_pair, "out_proj_pair")
    to_3 = add_pair(out_own[3], out_pair, 3, [], BF16, [])
    from_3 = along(to_3, 1, "out_proj_3")
    to_1 = add_pair(out_own[2], out_pair, 2, [], BF16, [to_3])
    *inner_met[1:], query_3 = hand_on([*inner_met[1:], query_3], [], FLOPS)
    *inner_met[1:], query_3 = hand_on([*inner_met[1:], query_3], [out_pair])
    w_query_own = [w_query_own, query_3]
    w_query_pair = [across(w, f"w_query_pair_{i}") for i, w in enumerate(w_query_own)]

    blocks = feed(
        ranks, inner_met, w_query_own, w_query_pair, w_key, w_value, pair, [to_3, to_1]
    )
    to_2 = add_pair(out_own[1], out_pair, 1, [from_3], BF16, [blocks[1]])
    out_proj_grad = add_pair(
        out_own[0], out_pair, 0, [along(to_1, 1, "out_proj"), along(to_2, 2, "out_proj")], F32, []
    )
    blocks = [(0, blocks[0])] + [(k, swapped(x, PLANE, k, f"grads_{k}")) for k, x in zip(meets, blocks[1:])]
    grad_input = place_blocks(ranks, [blocks[0][1]], [0], pair, features, None)
    for k, block in blocks[1:]:
        grad_input = place_blocks(ranks, [block], [k], pair, features, grad_input)
    grad_input = hand_on([grad_input], [], FLOPS)[0]
    return (grad_input, out_proj_grad)


def solution(mesh):
    placed = (
        P(("dp", "context", "tensor"), None),
        P(("dp", "context"), "tensor"),
        P(("dp", "context"), "tensor"),
        P(("dp", "context"), None),
        P(("dp", "context"), None),
        P("tensor", ("dp", "context")),
        P("dp", None),
        P(("dp", "context"), "tensor"),
        P("tensor", ("dp", "context")),
        P(),
        P(),
    )
    return jax.shard_map(
        on_device,
        mesh=mesh,
        in_specs=placed,
        out_specs=(P(("dp", "context", "tensor"), None), P(("dp", "context"), "tensor")),
        check_vma=False,
    )
```

```python
import functools
import math

import jax
import jax.numpy as jnp
from jax import lax
from jax.experimental import pallas as pl
from jax.experimental.pallas import tpu as pltpu
from jax.sharding import PartitionSpec as P

PLANE = ("dp", "context")
BF16 = jnp.bfloat16
F32 = jnp.float32
TENSOR_ORDER = (0, 2, 1, 3)


def swapped(x, axes, bit, name):
    size = lax.axis_size(axes)
    with jax.named_scope(name):
        return lax.ppermute(x, axes, [(i, i ^ bit) for i in range(size)])


def neighbours(to_left, to_right):
    size = lax.axis_size("context")
    up = [(i, i + 1) for i in range(size - 1)]
    down = [(i + 1, i) for i in range(size - 1)]
    return [lax.ppermute(to_right, "context", up), lax.ppermute(to_left, "context", down)]


def contract(x, y, dims):
    return lax.dot_general(x, y, (dims, ((), ())), preferred_element_type=F32)


VMEM = pl.BlockSpec(memory_space=pltpu.VMEM)
ANY = pl.BlockSpec(memory_space=pl.ANY)
FLOPS = 4 * 10**10
SMALL = pl.CostEstimate(flops=0, bytes_accessed=0, transcendentals=0)


def cut_kernel(
    ranks_ref, x_ref, key_ref, value_ref, weight_ref, *refs, parts, pair, width, carrier
):
    out_refs, weight_out_ref, sems = refs[:-2], refs[-2], refs[-1]
    moves = [(weight_ref, weight_out_ref)]
    for i, k in enumerate(parts):
        for half in range(2):
            owner = lax.bitwise_xor(ranks_ref[0], k ^ (half * pair))
            start = pl.multiple_of(owner * width, width)
            moves.append(
                (x_ref.at[:, pl.ds(start, width)], out_refs[i].at[:, half * width : (half + 1) * width])
            )
    if carrier is not None:
        rows, start = x_ref.shape[0], 2 * width
        for half in range(2):
            at = pl.ds(pl.multiple_of((2 * ranks_ref[2] + half) * rows, rows), rows)
            for ref in (key_ref, value_ref):
                end = start + ref.shape[1]
                moves.append((ref.at[at, :], out_refs[carrier].at[:, start:end]))
                start = end
    copies = [pltpu.make_async_copy(x, y, sems.at[i]) for i, (x, y) in enumerate(moves)]
    for copy in copies:
        copy.start()
    for copy in copies:
        copy.wait()


def cut(ranks, x, keys, values, weight, parts, pair, carrier):
    rows, width = x.shape[0], weight.shape[0]
    extra = 2 * (keys.shape[1] + values.shape[1])
    return pl.pallas_call(
        functools.partial(cut_kernel, parts=parts, pair=pair, width=width, carrier=carrier),
        out_shape=[
            jax.ShapeDtypeStruct((rows, 2 * width + (extra if i == carrier else 0)), x.dtype)
            for i in range(len(parts))
        ]
        + [jax.ShapeDtypeStruct(weight.shape, weight.dtype)],
        in_specs=[pl.BlockSpec(memory_space=pltpu.SMEM)] + [ANY] * 4,
        out_specs=[VMEM] * (len(parts) + 1),
        scratch_shapes=[pltpu.SemaphoreType.DMA((2 * len(parts) + 5,))],
        compiler_params=pltpu.CompilerParams(vmem_limit_bytes=60 * 2**20),
        cost_estimate=SMALL,
        name="cut",
    )(ranks, x, keys, values, weight)


def project_kernel(*refs, tokens, pieces, carrier):
    token_refs, refs = refs[:tokens], refs[tokens:]
    own_refs, pair_refs, refs = refs[:pieces], refs[pieces : 2 * pieces], refs[2 * pieces :]
    out_refs, held = refs[:tokens], refs[-1]
    rows = token_refs[0].shape[0]
    width, cols = own_refs[0].shape
    for i, ref in enumerate(token_refs):
        held[i * rows : (i + 1) * rows, :] = ref[:, : 2 * width]
    if carrier is not None:
        before_ref = refs[tokens]
        depth = before_ref.shape[1]
        for half in range(2):
            start = 2 * width + half * depth
            before_ref[half * rows : (half + 1) * rows, :] = token_refs[carrier][
                :, start : start + depth
            ]
    for j in range(pieces):
        total = contract(held[:, :width], own_refs[j][...], ((1,), (0,)))
        total = total + contract(held[:, width:], pair_refs[j][...], ((1,), (0,)))
        for i, ref in enumerate(out_refs):
            ref[:, j * cols : (j + 1) * cols] = total[i * rows : (i + 1) * rows].astype(ref.dtype)


def project(tokens, own, pair, carrier):
    rows = tokens[0].shape[0]
    width, cols = own[0].shape
    out_shape = [
        jax.ShapeDtypeStruct((rows, len(own) * cols), BF16 if i else F32)
        for i in range(len(tokens))
    ]
    if carrier is not None:
        extra = (tokens[carrier].shape[1] - 2 * width) // 2
        out_shape.append(jax.ShapeDtypeStruct((2 * rows, extra), BF16))
    return pl.pallas_call(
        functools.partial(
            project_kernel, tokens=len(tokens), pieces=len(own), carrier=carrier
        ),
        out_shape=out_shape,
        in_specs=[VMEM] * (len(tokens) + 2 * len(own)),
        out_specs=[VMEM] * len(out_shape),
        scratch_shapes=[pltpu.VMEM((rows * len(tokens), 2 * width), BF16)],
        compiler_params=pltpu.CompilerParams(vmem_limit_bytes=20 * 2**20),
        cost_estimate=SMALL,
        name="project",
    )(*tokens, *own, *pair)


def hand_on_kernel(*refs):
    pass


def hand_on(arrays, behind, flops=0):
    return pl.pallas_call(
        hand_on_kernel,
        out_shape=[jax.ShapeDtypeStruct(x.shape, x.dtype) for x in arrays],
        in_specs=[ANY] * (len(arrays) + len(behind)),
        out_specs=[ANY] * len(arrays),
        input_output_aliases={i: i for i in range(len(arrays))},
        compiler_params=pltpu.CompilerParams(vmem_limit_bytes=16 * 2**20),
        cost_estimate=pl.CostEstimate(flops=flops, bytes_accessed=0, transcendentals=0),
        name="hand_on",
    )(*arrays, *behind)


def add_kernel(ranks_ref, own_ref, att_ref, *refs, parts):
    part_refs, out_refs, share_refs = refs[:parts], refs[parts : -4], refs[-4:]
    rows, cols = out_refs[0].shape
    total = own_ref[...]
    for ref in part_refs:
        total = total + ref[...].astype(F32)
    for j, ref in enumerate(out_refs):
        ref[...] = total[:, j * cols : (j + 1) * cols].astype(BF16)
    for j, ref in zip(TENSOR_ORDER, share_refs):
        owner = lax.bitwise_xor(ranks_ref[1], j)
        ref[...] = att_ref[pl.ds(pl.multiple_of(owner * rows, rows), rows), :]


def add_up(ranks, own, attended, parts):
    rows, cols = own.shape[0], attended.shape[1]
    peers = len(TENSOR_ORDER)
    return pl.pallas_call(
        functools.partial(add_kernel, parts=len(parts)),
        out_shape=[jax.ShapeDtypeStruct((rows, cols), BF16)] * (2 * peers),
        in_specs=[pl.BlockSpec(memory_space=pltpu.SMEM)] + [VMEM] * (2 + len(parts)),
        out_specs=[VMEM] * (2 * peers),
        compiler_params=pltpu.CompilerParams(vmem_limit_bytes=60 * 2**20),
        cost_estimate=SMALL,
        name="add_up",
    )(ranks, own, attended, *parts)


def join_kernel(ranks_ref, kv_ref, *refs, backs, atts):
    back_refs, att_refs = refs[:backs], refs[backs : backs + atts]
    (away_ref, next_ref, own_ref, att_own_ref), held = refs[-5:-1], refs[-1]
    cols = att_refs[0].shape[1]
    for i, ref in enumerate(att_refs):
        att_own_ref[:, i * cols : (i + 1) * cols] = ref[...]
    rows = own_ref.shape[0]
    span = kv_ref.shape[0] // 2
    held[...] = kv_ref[...]
    if backs == 1:
        at = pl.ds(pl.multiple_of(ranks_ref[2] * span, span), span)
        held[at, :] = held[at, :] + back_refs[0][...].astype(F32)
    else:
        held[span:, :] = held[span:, :] + back_refs[0][...].astype(F32)
        held[:span, :] = held[:span, :] + back_refs[1][...].astype(F32)

    def rank_rows(j):
        at = pl.ds(pl.multiple_of(lax.bitwise_xor(ranks_ref[1], j) * rows, rows), rows)
        return held[at, :]

    away_ref[:rows, :] = rank_rows(2).astype(BF16)
    away_ref[rows:, :] = rank_rows(3).astype(BF16)
    next_ref[...] = rank_rows(1)
    own_ref[...] = rank_rows(0)


def join(ranks, kv, back, atts, behind):
    rows, width = kv.shape[0] // len(TENSOR_ORDER), kv.shape[1]
    return pl.pallas_call(
        functools.partial(join_kernel, backs=len(back), atts=len(atts)),
        out_shape=[
            jax.ShapeDtypeStruct((2 * rows, width), BF16),
            jax.ShapeDtypeStruct((rows, width), F32),
            jax.ShapeDtypeStruct((rows, width), F32),
            jax.ShapeDtypeStruct((rows, len(atts) * atts[0].shape[1]), BF16),
        ],
        in_specs=[pl.BlockSpec(memory_space=pltpu.SMEM)]
        + [VMEM] * (1 + len(back) + len(atts))
        + [ANY] * len(behind),
        out_specs=[VMEM] * 4,
        scratch_shapes=[pltpu.VMEM(kv.shape, F32)],
        compiler_params=pltpu.CompilerParams(vmem_limit_bytes=8 * 2**20),
        cost_estimate=SMALL,
        name="join",
    )(ranks, kv, *back, *atts, *behind)


def inner_kernel(rest_ref, got_ref, next_ref, *refs, pieces):
    query_refs, out_ref = refs[:pieces], refs[-2]
    rows, cols = query_refs[0].shape
    for i, ref in enumerate(query_refs):
        out_ref[:, i * cols : (i + 1) * cols] = ref[...]
    kv = rest_ref[...] + got_ref[:rows, :].astype(F32) + next_ref[...].astype(F32)
    out_ref[:, pieces * cols :] = kv.astype(BF16)


def inner_grads(rest, got, from_next, queries, later, behind):
    rows, cols = queries[0].shape
    return pl.pallas_call(
        functools.partial(inner_kernel, pieces=len(queries)),
        out_shape=[
            jax.ShapeDtypeStruct((rows, cols * len(queries) + rest.shape[1]), BF16),
            jax.ShapeDtypeStruct(later.shape, later.dtype),
        ],
        in_specs=[VMEM] * (3 + len(queries)) + [ANY] * (1 + len(behind)),
        out_specs=[VMEM, ANY],
        input_output_aliases={3 + len(queries): 1},
        compiler_params=pltpu.CompilerParams(vmem_limit_bytes=8 * 2**20),
        cost_estimate=SMALL,
        name="inner",
    )(rest, got, from_next, *queries, later, *behind)


def outer_kernel(*refs, tokens, atts, weights):
    held, att_held = refs[-2:]
    *own_refs, pair_ref, whole_ref = refs[-4 - len(TENSOR_ORDER) : -2]
    width, cols = own_refs[0].shape
    weight_refs = refs[tokens + atts : tokens + atts + weights]
    for block_refs, whole in (
        (refs[:tokens], held), (refs[tokens : tokens + atts], att_held), (weight_refs, whole_ref),
    ):
        start, columns = 0, whole.shape[1]
        for ref in block_refs:
            whole[start : start + ref.shape[0], :] = ref[:, :columns]
            start += ref.shape[0]
    step = min(width, 256)
    for e in range(0, width, step):
        at = slice(e, e + step)
        total = contract(held[:, at], att_held[...], ((0,), (0,)))
        for j, ref in enumerate(own_refs):
            ref[at, :] = total[:, j * cols : (j + 1) * cols]
        pair_at = slice(width + e, width + e + step)
        pair_ref[at, :] = contract(held[:, pair_at], att_held[...], ((0,), (0,))).astype(BF16)


def outer(tokens, atts, weights, behind):
    width, columns = weights[0].shape[1], atts[0].shape[1]
    depth, cols = tokens[0].shape[0] * len(tokens), columns // len(TENSOR_ORDER)
    return pl.pallas_call(
        functools.partial(
            outer_kernel, tokens=len(tokens), atts=len(atts), weights=len(weights)
        ),
        out_shape=[jax.ShapeDtypeStruct((width, cols), F32)] * len(TENSOR_ORDER)
        + [
            jax.ShapeDtypeStruct((width, columns), BF16),
            jax.ShapeDtypeStruct((sum(w.shape[0] for w in weights), width), BF16),
        ],
        in_specs=[VMEM] * (len(tokens) + len(atts) + len(weights)) + [ANY] * len(behind),
        out_specs=[VMEM] * (len(TENSOR_ORDER) + 2),
        scratch_shapes=[pltpu.VMEM((depth, 2 * width), BF16), pltpu.VMEM((depth, columns), BF16)],
        compiler_params=pltpu.CompilerParams(vmem_limit_bytes=14 * 2**20),
        cost_estimate=SMALL,
        name="outer",
    )(*tokens, *atts, *weights, *behind)


def add_pair_kernel(*refs, addends):
    own_ref, pair_ref, out_ref = refs[0], refs[1], refs[-1]
    total = own_ref[...] + pair_ref[...].astype(F32)
    for ref in refs[2:addends]:
        total = total + ref[...].astype(F32)
    out_ref[...] = total.astype(out_ref.dtype)


def add_pair(own, pair, block, others, dtype, behind):
    columns = pl.BlockSpec(own.shape, lambda i: (0, block))
    whole = pl.BlockSpec(own.shape, lambda i: (0, 0))
    return pl.pallas_call(
        functools.partial(add_pair_kernel, addends=2 + len(others)),
        grid=(1,),
        out_shape=jax.ShapeDtypeStruct(own.shape, dtype),
        in_specs=[whole, columns] + [whole] * len(others) + [ANY] * len(behind),
        out_specs=whole,
        compiler_params=pltpu.CompilerParams(vmem_limit_bytes=8 * 2**20),
        cost_estimate=SMALL,
        name="add_pair",
    )(own, pair, *others, *behind)


def feed_kernel(ranks_ref, *refs, tokens, pieces, distance):
    inner_refs, refs = refs[:tokens], refs[tokens:]
    weights, refs = [refs[i * pieces : (i + 1) * pieces] for i in range(2)], refs[2 * pieces :]
    out_refs, (held, last, sems) = refs[-3 - tokens : -3], refs[-3:]
    rows, columns = inner_refs[0].shape
    width = last.shape[1] // 2
    depth = refs[0].shape[0]
    copies = []
    for half in range(2):
        owner = lax.bitwise_xor(ranks_ref[0], half * distance)
        at = pl.ds(pl.multiple_of(owner * width, width), width)
        for i, ref in enumerate(refs[:2]):
            copies.append(
                pltpu.make_async_copy(
                    ref.at[:, at],
                    last.at[i * depth : (i + 1) * depth, half * width : (half + 1) * width],
                    sems.at[2 * half + i],
                )
            )
    for copy in copies:
        copy.start()
    for i, ref in enumerate(inner_refs):
        held[i * rows : (i + 1) * rows, :] = ref[...]
    for copy in copies:
        copy.wait()
    step = min(width, 512)
    for half in range(2):
        for start in range(0, width, step):
            at = slice(half * width + start, half * width + start + step)
            total = contract(held[:, columns - 2 * depth :], last[:, at], ((1,), (0,)))
            done = 0
            for w in weights[half]:
                part = held[:, done : done + w.shape[0]]
                total = total + contract(part, w[:, start : start + step], ((1,), (0,)))
                done += w.shape[0]
            for i, ref in enumerate(out_refs):
                ref[:, at] = total[i * rows : (i + 1) * rows].astype(BF16)


def feed(ranks, inners, own, pair, w_key, w_value, distance, behind):
    rows, columns = inners[0].shape
    width = own[0].shape[1]
    return pl.pallas_call(
        functools.partial(feed_kernel, tokens=len(inners), pieces=len(own), distance=distance),
        out_shape=[jax.ShapeDtypeStruct((rows, 2 * width), BF16)] * len(inners),
        in_specs=[pl.BlockSpec(memory_space=pltpu.SMEM)]
        + [VMEM] * (len(inners) + 2 * len(own))
        + [ANY] * (2 + len(behind)),
        out_specs=[VMEM] * len(inners),
        scratch_shapes=[
            pltpu.VMEM((rows * len(inners), columns), BF16),
            pltpu.VMEM((2 * w_key.shape[0], 2 * width), BF16),
            pltpu.SemaphoreType.DMA((4,)),
        ],
        compiler_params=pltpu.CompilerParams(vmem_limit_bytes=14 * 2**20),
        cost_estimate=SMALL,
        name="feed",
    )(ranks, *inners, *own, *pair, w_key, w_value, *behind)


def place_kernel(ranks_ref, *refs, parts, distance):
    out_ref, sems = refs[-2], refs[-1]
    width = refs[0].shape[1] // 2
    copies = []
    for i, (k, ref) in enumerate(zip(parts, refs)):
        for half in range(2):
            owner = lax.bitwise_xor(ranks_ref[0], k ^ (half * distance))
            at = pl.ds(pl.multiple_of(owner * width, width), width)
            copies.append(
                pltpu.make_async_copy(
                    ref.at[:, half * width : (half + 1) * width],
                    out_ref.at[:, at],
                    sems.at[2 * i + half],
                )
            )
    for copy in copies:
        copy.start()
    for copy in copies:
        copy.wait()


def place_blocks(ranks, blocks, parts, distance, features, out):
    given = [] if out is None else [out]
    return pl.pallas_call(
        functools.partial(place_kernel, parts=parts, distance=distance),
        out_shape=jax.ShapeDtypeStruct((blocks[0].shape[0], features), BF16),
        in_specs=[pl.BlockSpec(memory_space=pltpu.SMEM)]
        + [VMEM] * len(blocks)
        + [ANY] * len(given),
        out_specs=ANY,
        scratch_shapes=[pltpu.SemaphoreType.DMA((2 * len(blocks),))],
        input_output_aliases={1 + len(blocks): 0} if given else {},
        compiler_params=pltpu.CompilerParams(vmem_limit_bytes=4 * 2**20),
        cost_estimate=SMALL,
        name="place",
    )(ranks, *blocks, *given)


def attention_kernel(
    ranks_ref, seg_query_ref, seg_key_ref, query_ref, attended_ref, key_ref, value_ref, log_ref,
    *refs, peers, befores, cycle_size,
):
    dout_refs, before_refs = refs[:peers], refs[peers : peers + befores]
    dquery_refs, away_refs = refs[-3 - befores - peers : -3 - befores], refs[-3 - befores : -3]
    kv_grads_ref, dout_held, dquery_held = refs[-3:]
    rank, last_rank = ranks_ref[1], ranks_ref[2] == cycle_size - 1
    head_dim = key_ref.shape[1]
    span = query_ref.shape[0] // 2
    heads = query_ref.shape[1] // head_dim
    sub = 2 * span // peers
    inv_root = 1.0 / math.sqrt(head_dim)

    def place(a):
        return pl.ds(pl.multiple_of(a * sub, sub), sub)

    def by_head(x):
        return jnp.concatenate(
            [x[:, h * head_dim : (h + 1) * head_dim] for h in range(heads)], axis=0
        )

    for j, ref in zip(TENSOR_ORDER, dout_refs):
        dout_held[place(lax.bitwise_xor(rank, j)), :] = ref[...]
    before = []
    for b in range(2):
        rows = slice(b * span, (b + 1) * span)
        query = by_head(query_ref[rows, :])
        dout = by_head(dout_held[rows, :])
        attended = by_head(attended_ref[rows, :])
        key_before = before_refs[b % befores][:, :head_dim]
        value_before = before_refs[b % befores][:, head_dim:]
        if b == 1:
            key_before = jnp.where(last_rank, key_ref[:span, :], key_before)
            value_before = jnp.where(last_rank, value_ref[:span, :], value_before)
        key = jnp.concatenate([key_before, key_ref[rows, :]], axis=0)
        value = jnp.concatenate([value_before, value_ref[rows, :]], axis=0)
        log_rows = jnp.concatenate([log_ref[rows, h : h + 1] for h in range(heads)], axis=0)
        query_at = lax.broadcasted_iota(jnp.int32, (span, 2 * span), 0)
        key_at = lax.broadcasted_iota(jnp.int32, (span, 2 * span), 1) - span
        allowed = (key_at <= query_at) & (seg_query_ref[rows, :] == seg_key_ref[b : b + 1, :])
        allowed = jnp.concatenate([allowed] * heads, axis=0)
        scores = contract(query, key, ((1,), (1,))) * inv_root
        prob = jnp.where(allowed, jnp.exp(scores - log_rows), 0.0)
        delta = jnp.sum(dout.astype(F32) * attended.astype(F32), axis=1, keepdims=True)
        dprob = contract(dout, value, ((1,), (1,)))
        dscore = (prob * (dprob - delta)).astype(BF16)
        dquery = (contract(dscore, key, ((1,), (0,))) * inv_root).astype(BF16)
        for h in range(heads):
            dquery_held[rows, h * head_dim : (h + 1) * head_dim] = dquery[
                h * span : (h + 1) * span
            ]
        key_grads = contract(dscore, query, ((0,), (0,))) * inv_root
        value_grads = contract(prob.astype(BF16), dout, ((0,), (0,)))
        kv_grads_ref[rows, :head_dim] = key_grads[span:]
        kv_grads_ref[rows, head_dim:] = value_grads[span:]
        before.append((key_grads[:span], value_grads[:span]))
    for i, half in enumerate((slice(0, head_dim), slice(head_dim, 2 * head_dim))):
        low, high = before[0][i], before[1][i]
        kv_grads_ref[:span, half] = kv_grads_ref[:span, half] + jnp.where(last_rank, high, 0.0)
        if befores == 1:
            away_refs[0][:, half] = jnp.where(last_rank, low, high).astype(BF16)
        else:
            away_refs[0][:, half] = low.astype(BF16)
            away_refs[1][:, half] = jnp.where(last_rank, 0.0, high).astype(BF16)
    for j, ref in zip(TENSOR_ORDER, dquery_refs):
        ref[...] = dquery_held[place(lax.bitwise_xor(rank, j)), :]


def attention(
    ranks, seg_query, seg_key, queries, attended, keys, values, log_sums, dout, before, behind,
    cycle_size,
):
    kv_shape = (keys.shape[0], 2 * keys.shape[1])
    return pl.pallas_call(
        functools.partial(
            attention_kernel, peers=len(dout), befores=len(before), cycle_size=cycle_size
        ),
        out_shape=[jax.ShapeDtypeStruct(dout[0].shape, BF16) for _ in dout]
        + [jax.ShapeDtypeStruct(x.shape, BF16) for x in before]
        + [jax.ShapeDtypeStruct(kv_shape, F32)],
        in_specs=[pl.BlockSpec(memory_space=pltpu.SMEM)]
        + [VMEM] * (7 + len(dout) + len(before))
        + [ANY] * len(behind),
        out_specs=[VMEM] * (len(dout) + len(before) + 1),
        scratch_shapes=[pltpu.VMEM(queries.shape, BF16)] * 2,
        compiler_params=pltpu.CompilerParams(vmem_limit_bytes=32 * 2**20),
        cost_estimate=SMALL,
        name="attention",
    )(ranks, seg_query, seg_key, queries, attended, keys, values, log_sums, *dout, *before, *behind)


def on_device(
    grad_out, queries, attended, keys, values, log_sums, segment_ids, w_out, w_query, w_key, w_value
):
    tensor_rank = lax.axis_index("tensor")
    plane_rank = lax.axis_index(PLANE)
    cycle_size, cycle_pos = lax.axis_size("context"), lax.axis_index("context")
    own_rows, features = grad_out.shape
    width = w_out.shape[0]
    cols = queries.shape[1]
    span = queries.shape[0] // 2
    pair = cycle_size
    bits = [1 << i for i in range(lax.axis_size(PLANE).bit_length() - 1)]
    bits = [bit for bit in reversed(bits) if bit != pair]
    meets = [0]
    for bit in bits:
        meets += [k ^ bit for k in meets]
    meets = meets[1:]

    def plane_gather(x, name):
        return [x] + [swapped(x, PLANE, k, f"{name}_{k}") for k in meets]

    def along(x, j, name):
        return swapped(x, "tensor", j, f"{name}_{j}")

    def across(x, name):
        return swapped(x, PLANE, pair, name)

    out_2, out_1 = along(w_out, 2, "w_out"), along(w_out, 1, "w_out")

    ranks = jnp.stack([plane_rank, tensor_rank, cycle_pos])
    carrier = meets.index(1) + 1 if cycle_size == 2 else None
    *tokens, w_out_copy = cut(ranks, grad_out, keys, values, w_out, [0] + meets, pair, carrier)
    tokens = [tokens[0]] + [swapped(x, PLANE, k, f"tokens_{k}") for k, x in zip(meets, tokens[1:])]
    out_2, out_1 = hand_on([out_2, out_1], [], FLOPS // 10)
    out_2, w_out_copy = hand_on([out_2, w_out_copy], tokens[1:2])
    out_1 = hand_on([out_1], tokens[2:], FLOPS)[0]
    w_out_own = [w_out_copy, out_2, out_1, along(out_2, 1, "w_out_on")]
    w_out_pair = [across(w, f"w_out_pair_{i}") for i, w in enumerate(w_out_own)]

    query_2, query_1 = along(w_query, 2, "w_query"), along(w_query, 1, "w_query")
    query_2, query_1 = hand_on([query_2, query_1], [], FLOPS // 10)

    seg_row = segment_ids[0]
    high_span = 2 * cycle_size - 1 - cycle_pos

    def seg_slice(at):
        return lax.dynamic_slice_in_dim(seg_row, jnp.maximum(at, 0) * span, span)

    seg_low, seg_high = seg_slice(cycle_pos), seg_slice(high_span)
    seg_before = jnp.where(cycle_pos == 0, -1, seg_slice(cycle_pos - 1))
    seg_query = jnp.concatenate([seg_low, seg_high])[:, None]
    seg_key = jnp.stack(
        [
            jnp.concatenate([seg_before, seg_low]),
            jnp.concatenate([seg_slice(high_span - 1), seg_high]),
        ]
    )
    log_rows = log_sums.T

    partial_attn = project(tokens, w_out_own, w_out_pair, carrier)
    partial_attn, before = partial_attn[: len(tokens)], partial_attn[len(tokens) :]
    if cycle_size != 2:
        kv_pair = jnp.concatenate([keys, values], axis=1)
        before = neighbours(kv_pair[span:], kv_pair[:span])
    parts = [swapped(x, PLANE, k, f"attn_{k}") for k, x in zip(meets, partial_attn[1:])]
    shared = add_up(ranks, partial_attn[0], attended, parts)
    dout, atts = shared[:4], shared[4:]
    dout = [dout[0]] + [along(x, j, "dout") for x, j in zip(dout[1:], TENSOR_ORDER[1:])]
    dout[1:] = hand_on(dout[1:], [], FLOPS // 10)
    atts = [along(x, j, "attended") for x, j in zip(atts[1:], TENSOR_ORDER[1:])]
    atts = [shared[4], *hand_on(atts, [], FLOPS // 10)]
    *dquery, kv_grads = attention(
        ranks, seg_query, seg_key, queries, attended, keys, values, log_rows, dout, before,
        [query_2, query_1], cycle_size,
    )
    dquery, away = dquery[:4], dquery[4:]

    dquery = dquery[:1] + [along(x, j, "dquery") for x, j in zip(dquery[1:], TENSOR_ORDER[1:])]
    back = [swapped(away[0], "context", 1, "kv_back")] if cycle_size == 2 else neighbours(*away)
    kv_away, kv_next, kv_rest, att_own = join(ranks, kv_grads, back, atts, dquery[1:])
    att_met = plane_gather(att_own, "attended")
    att_met[1:] = hand_on(att_met[1:], [], FLOPS // 10)
    got = along(kv_away, 2, "kv")
    kv_next = along((kv_next + got[own_rows:].astype(F32)).astype(BF16), 1, "kv")
    inner, query_2 = inner_grads(
        kv_rest, got, kv_next, dquery, query_2, []
    )
    inner_met = plane_gather(inner, "inner")

    *out_own, out_pair, w_query_own = outer(
        tokens, att_met, [w_query, query_2, query_1], [inner]
    )
    query_3 = along(query_2, 1, "w_query_on")

    out_pair = across(out_pair, "out_proj_pair")
    to_3 = add_pair(out_own[3], out_pair, 3, [], BF16, [])
    from_3 = along(to_3, 1, "out_proj_3")
    to_1 = add_pair(out_own[2], out_pair, 2, [], BF16, [to_3])
    *inner_met[1:], query_3 = hand_on([*inner_met[1:], query_3], [], FLOPS)
    *inner_met[1:], query_3 = hand_on([*inner_met[1:], query_3], [out_pair])
    w_query_own = [w_query_own, query_3]
    w_query_pair = [across(w, f"w_query_pair_{i}") for i, w in enumerate(w_query_own)]

    blocks = feed(
        ranks, inner_met, w_query_own, w_query_pair, w_key, w_value, pair, [to_3, to_1]
    )
    to_2 = add_pair(out_own[1], out_pair, 1, [from_3], BF16, [blocks[1]])
    out_proj_grad = add_pair(
        out_own[0], out_pair, 0, [along(to_1, 1, "out_proj"), along(to_2, 2, "out_proj")], F32, []
    )
    blocks = [(0, blocks[0])] + [(k, swapped(x, PLANE, k, f"grads_{k}")) for k, x in zip(meets, blocks[1:])]
    grad_input = place_blocks(ranks, [blocks[0][1]], [0], pair, features, None)
    for k, block in blocks[1:]:
        grad_input = place_blocks(ranks, [block], [k], pair, features, grad_input)
    grad_input = hand_on([grad_input], [], FLOPS)[0]
    return (grad_input, out_proj_grad)


def solution(mesh):
    placed = (
        P(("dp", "context", "tensor"), None),
        P(("dp", "context"), "tensor"),
        P(("dp", "context"), "tensor"),
        P(("dp", "context"), None),
        P(("dp", "context"), None),
        P("tensor", ("dp", "context")),
        P("dp", None),
        P(("dp", "context"), "tensor"),
        P("tensor", ("dp", "context")),
        P(),
        P(),
    )
    return jax.shard_map(
        on_device,
        mesh=mesh,
        in_specs=placed,
        out_specs=(P(("dp", "context", "tensor"), None), P(("dp", "context"), "tensor")),
        check_vma=False,
    )
```
